512 devices in a mesh: dp: 128 (over x, z, core), tensor: 4 (over y).
Axes of the slice: x: 4, y: 4, z: 16, core: 2. Of those that a mesh axis runs over, the one named last changes fastest.
Arguments:
- grad: bfloat16 [48, 1441792], P(None, ('dp', 'tensor')), may hold values from -100 to 100
- momentum: float32 [48, 1441792], P(None, ('dp', 'tensor')), may hold values from -6 to 6
- owner: int32 [48], replicated, may hold values from 0 to 127, as said below
Outputs:
- new_momentum: float32 [48, 1441792], P(None, ('dp', 'tensor'))
- update: bfloat16 [48, 1441792], P(None, ('dp', 'tensor'))
- owned_rms: float32 [128, 2], P('dp')
The draws below stay inside these ranges and needn't reach their ends.
Inputs may be any that keep to these rules, and one draw needn't show every extreme that they name: `owner`: each matrix's owning dp index; no index owns more than 2 matrices, and some index owns exactly 2.
All inputs are finite; a program needn't handle non-finite values.
Results may differ from the reference program's by a relative error of at most 0.012.
Values may be sent and summed in bfloat16 or wider, within the bound.
A program may use at most 64 MiB of HBM per device.

```python
import math
import jax
import jax.numpy as jnp
from jax import lax

D = 2048
HW = 704
ITERS = 2
MATS = 48
CAP = 2
N_DP = 128
N_TENSOR = 4


def draw_grad(key, part):
    key = jax.random.fold_in(key, 7)
    key_base, key_rows, key_cols = jax.random.split(key, 3)
    base = jnp.clip(jax.random.normal(key_base, (MATS, D, HW), jnp.float32), -4.0, 4.0)
    row_scale = jnp.exp(jax.random.uniform(key_rows, (MATS, D, 1), jnp.float32) * math.log(10.0))
    col_scale = jnp.exp(jax.random.uniform(key_cols, (MATS, 1, HW), jnp.float32) * math.log(10.0))
    return (base * row_scale * col_scale * 0.25).reshape(MATS, D * HW).astype(jnp.bfloat16)


def draw_owner(key, part):
    key = jax.random.fold_in(key, 11)
    key_owners, key_slots, key_order = jax.random.split(key, 3)
    owners_order = jax.random.permutation(key_owners, N_DP).astype(jnp.int32)
    free_slots = jax.random.permutation(key_slots, (N_DP - 1) * CAP).astype(jnp.int32)[:MATS - CAP]
    others = owners_order[1 + free_slots // CAP]
    first = jnp.full((CAP,), owners_order[0], jnp.int32)
    sequence = jnp.concatenate([first, others])
    placing = jax.random.permutation(key_order, MATS).astype(jnp.int32)
    return jnp.zeros((MATS,), jnp.int32).at[placing].set(sequence)


def block_scale(stream_key, shape, cuts, smallest, high):
    def one(dim, parts):
        heights = jax.random.uniform(jax.random.fold_in(jax.random.fold_in(stream_key, 6), dim), (parts,), jnp.float32, smallest / len(cuts), high / len(cuts))
        return jnp.repeat(jnp.exp(heights), shape[dim] // parts).reshape((-1,) + (1,) * (len(shape) - dim - 1))

    factor_of = one(*cuts[0])
    for cut in cuts[1:]:
        factor_of = factor_of * one(*cut)
    return factor_of


def bell_draw(own_key, dims, width, reach, cuts=(), held_as=jnp.bfloat16):
    gain = block_scale(own_key, dims, cuts, -0.22, 0.18) if cuts else 1.0
    result = jax.random.normal(own_key, dims, jnp.float32) * width * gain
    return jnp.minimum(jnp.maximum(result, -reach), reach).astype(held_as)


def setup_inputs(seed: int = 0) -> dict:
    arg_keys = jax.random.split(jax.random.key(seed), 4)
    grad = draw_grad(jax.random.fold_in(arg_keys[3], 71), 0)
    momentum = bell_draw(arg_keys[1], (MATS, D * HW), 1.0, 6.0, ((1, 512),), jnp.float32)
    owner = draw_owner(jax.random.fold_in(arg_keys[3], 71), 0)
    return {"grad": grad, "momentum": momentum, "owner": owner}


beta_decay = 0.95
coef_a = 3.4445
coef_b = -4.775
coef_c = 2.0315
epsilon = 1e-07

def part_gram(matrix):
    sub_rows = D // (N_DP * N_TENSOR)
    pieces = matrix.astype(jnp.float32).reshape(N_DP, N_TENSOR, sub_rows, HW)
    partial_value = jnp.einsum('iush,iusk->uhk', pieces, pieces, precision=lax.Precision.HIGHEST)
    rounded = lax.optimization_barrier(partial_value.astype(jnp.bfloat16))
    return lax.optimization_barrier(jnp.sum(rounded.astype(jnp.float32), axis=0))

def orthogonal(flat_matrix):
    nesterov = flat_matrix.reshape(D, HW)
    first = part_gram(nesterov)
    squares = jnp.trace(first)
    inverse = 1.0 / (jnp.sqrt(squares) + epsilon)
    scale_out = math.sqrt(max(D, HW))
    current = (first * inverse * inverse).astype(jnp.bfloat16)
    iterate = nesterov
    for iteration in range(ITERS):
        if iteration > 0:
            current = part_gram(iterate).astype(jnp.bfloat16)
        square = jnp.dot(current, current, preferred_element_type=jnp.float32)
        poly = (coef_b * current.astype(jnp.float32) + coef_c * square).astype(jnp.bfloat16)
        mixed = coef_a * iterate.astype(jnp.float32) + jnp.dot(iterate, poly, preferred_element_type=jnp.float32)
        if iteration == 0:
            mixed = mixed * inverse
        if iteration == ITERS - 1:
            mixed = mixed * scale_out
        iterate = mixed.astype(jnp.bfloat16)
    return (iterate.reshape(D * HW), jnp.sqrt(squares / (D * HW)))

def reference(grad, momentum, owner):
    new_momentum = beta_decay * momentum + grad.astype(jnp.float32)
    nesterov = (grad.astype(jnp.float32) + beta_decay * new_momentum).astype(jnp.bfloat16)
    update, matrix_rms = lax.map(orthogonal, nesterov)
    index = jnp.arange(MATS, dtype=jnp.int32)
    same_owner = owner[:, None] == owner[None, :]
    owner_rank = lax.optimization_barrier(jnp.sum((same_owner & (index[:, None] < index[None, :])).astype(jnp.int32), axis=0))
    owners = jnp.arange(N_DP, dtype=jnp.int32)
    slots = jnp.arange(CAP, dtype=jnp.int32)
    selector = ((owner[None, None, :] == owners[:, None, None]) & (owner_rank[None, None, :] == slots[None, :, None])).astype(jnp.float32)
    owned_rms = jnp.einsum('osm,m->os', selector, matrix_rms, precision=lax.Precision.HIGHEST)
    return (new_momentum, update, owned_rms)
```

```python
import math

import jax
import jax.numpy as jnp
from jax import lax
from jax.experimental import pallas as pl
from jax.experimental.pallas import tpu as pltpu
from jax.sharding import PartitionSpec as P

HW = 704
WIDE = 768
D = 2048
MATS = 48
CAP = 2
N_DP = 128
N_TENSOR = 4
SUB = 4
PLANE = N_DP // 2
PER_Y = MATS // N_TENSOR
BAND = SUB * N_TENSOR
ROWS = PLANE * BAND
TILE = 256

beta_decay = 0.95
coef_a = 3.4445
coef_b = -4.775
coef_c = 2.0315
epsilon = 1e-07

MESH = pl.DeviceIdType.MESH
f32, bf16 = jnp.float32, jnp.bfloat16


def home(j):
    return (j % 4) * 16 + (j * 4) // 3


def around(i):
    return (i + 1) // 2 if i % 2 else -(i // 2)


def one_hot(size, source):
    out_row = lax.broadcasted_iota(jnp.int32, (size, size), 0)
    in_row = lax.broadcasted_iota(jnp.int32, (size, size), 1)
    return (in_row == source(out_row)).astype(f32).astype(bf16)


def permuted(matrix, value):
    return jnp.dot(matrix, value, preferred_element_type=f32).astype(bf16)


def kernel(
    grad_ref, momentum_ref, owner_ref, momentum_out, update_out, rms_out,
    staged, from_y, bands, rows, turned, mid, done, total, half, other, gram, poly, back, to_y, land,
    send_y, recv_y, send_p, recv_p, send_g, recv_g, send_b, recv_b, send_z, recv_z, local_y, local_z,
):
    dp, y = lax.axis_index("dp"), lax.axis_index("tensor")
    core, place = dp % 2, dp // 2
    x, z = place // 16, place % 16
    mine = (3 * z + 3) // 4
    works = ((mine * 4) // 3 == z) & (mine % 4 == x) & (mine < PER_Y)
    bands_per = TILE // BAND

    barrier = pltpu.get_barrier_semaphore()
    for step in range(1, N_TENSOR):
        pl.semaphore_signal(barrier, inc=1, device_id=(dp, (y + step) % N_TENSOR), device_id_type=MESH)

    @pl.when(works)
    def _():
        pl.semaphore_signal(barrier, inc=1, device_id=(dp + 1 - 2 * core, y), device_id_type=MESH)

        def greet(step, carry):
            peer = (place + step) % PLANE
            pl.semaphore_signal(barrier, inc=1, device_id=(peer * 2 + core, y), device_id_type=MESH)
            return carry

        lax.fori_loop(1, PLANE, greet, 0)

    @pl.when(jnp.logical_not(works))
    def _():
        for j in range(PER_Y):
            pl.semaphore_signal(barrier, inc=1, device_id=(home(j) * 2 + core, y), device_id_type=MESH)

    grad = grad_ref[...].astype(f32)
    new_momentum = beta_decay * momentum_ref[...] + grad
    momentum_out[...] = new_momentum
    nesterov = (grad + beta_decay * new_momentum).astype(bf16)
    edge = jnp.zeros((MATS, WIDE - HW), bf16)
    by_row = jnp.concatenate(
        [jnp.concatenate([nesterov[:, HW * r:HW * (r + 1)], edge], axis=1) for r in range(SUB)], axis=0
    )
    to_matrix = one_hot(MATS * SUB, lambda o: (o % SUB) * MATS + o // SUB)
    staged[...] = permuted(to_matrix, by_row).reshape(N_TENSOR, PER_Y * SUB, WIDE)

    @pl.when(works)
    def _():
        pl.semaphore_wait(barrier, N_TENSOR - 1 + 1 + PLANE - 1)

    @pl.when(jnp.logical_not(works))
    def _():
        pl.semaphore_wait(barrier, N_TENSOR - 1 + PER_Y)

    def tile_at(i):
        t = (jnp.minimum(mine // 4, 2) + i) % 3
        return t, pl.ds(pl.multiple_of(t * BAND, BAND), BAND)

    def y_copy(src, dst, step, i, sends, recvs):
        peer = (y + step) % N_TENSOR
        at = tile_at(i)[1]
        return pltpu.make_async_remote_copy(
            src_ref=src.at[peer, at], dst_ref=dst.at[y, at],
            send_sem=sends.at[step - 1, i], recv_sem=recvs.at[step - 1, i],
            device_id=(dp, peer), device_id_type=MESH,
        )

    own = pltpu.make_async_copy(staged.at[y], from_y.at[y], local_y)
    own.start()
    for i in range(3):
        for step in range(1, N_TENSOR):
            y_copy(staged, from_y, step, i, send_y, recv_y).start()
    own.wait()

    def band_copy(i, k):
        j = tile_at(i)[0] * 4 + k
        return pltpu.make_async_remote_copy(
            src_ref=bands.at[j], dst_ref=rows.at[place], send_sem=send_p.at[i, k], recv_sem=recv_p.at[x],
            device_id=(home(j) * 2 + core, y), device_id_type=MESH,
        )

    def stays(i, k):
        return works & (tile_at(i)[0] * 4 + k == mine)

    regroup = one_hot(4 * BAND, lambda o: (o // SUB % 4) * BAND + (o // BAND) * SUB + o % SUB)
    for i in range(3):
        for step in range(1, N_TENSOR):
            y_copy(staged, from_y, step, i, send_y, recv_y).wait_recv()
        t, at = tile_at(i)
        tile = from_y[:, at, :].reshape(4 * BAND, WIDE)
        bands[pl.ds(4 * t, 4)] = permuted(regroup, tile).reshape(4, BAND, WIDE)
        for k in range(4):
            @pl.when(jnp.logical_not(stays(i, k)))
            def _():
                band_copy(i, k).start()

    @pl.when(works)
    def _():
        pltpu.make_async_copy(bands.at[mine], rows.at[place], recv_p.at[x]).start()

        def turn(ref, b):
            at = pl.multiple_of(b * TILE, TILE)
            turned[:, pl.ds(at, TILE)] = ref[pl.ds(b * bands_per, bands_per)].reshape(TILE, WIDE).T

        def swap(slot, c):
            return pltpu.make_async_remote_copy(
                src_ref=half.at[slot, c], dst_ref=other.at[slot, c], send_sem=send_g.at[slot, c], recv_sem=recv_g.at[slot, c],
                device_id=(dp + 1 - 2 * core, y), device_id_type=MESH,
            )

        def gram_sum(ref, slot):
            for c in range(WIDE // TILE):
                right = ref[:, :, c * TILE:(c + 1) * TILE].reshape(ROWS, TILE)
                half[slot, c] = jnp.dot(turned[...], right, preferred_element_type=f32).astype(bf16)
                swap(slot, c).start()
            for c in range(WIDE // TILE):
                swap(slot, c).wait()
                total[:, c * TILE:(c + 1) * TILE] = half[slot, c].astype(f32) + other[slot, c].astype(f32)

        def polynomial():
            current = gram[...]
            square = jnp.dot(current, current, preferred_element_type=f32)
            poly[...] = (coef_b * current.astype(f32) + coef_c * square).astype(bf16)

        def arrive(i, carry):
            b = (x + i) % 4
            column = rows.at[pl.ds(b * bands_per, bands_per)]
            pltpu.make_async_copy(column, column, recv_p.at[b]).wait()
            turn(rows, b)
            return carry

        lax.fori_loop(0, ROWS // TILE, arrive, 0)
        gram_sum(rows, 0)
        diagonal = lax.broadcasted_iota(jnp.int32, (TILE, TILE), 0) == lax.broadcasted_iota(jnp.int32, (TILE, TILE), 1)
        on_diagonal = sum(
            jnp.where(diagonal, total[c * TILE:(c + 1) * TILE, c * TILE:(c + 1) * TILE], 0.0) for c in range(WIDE // TILE)
        )
        squares = jnp.sum(jnp.sum(on_diagonal, axis=1, keepdims=True), axis=0, keepdims=True)
        inverse = 1.0 / (jnp.sqrt(squares) + epsilon)
        gram[...] = (total[...] * inverse * inverse).astype(bf16)
        polynomial()

        current = rows[...].reshape(ROWS, WIDE)
        product = jnp.dot(current, poly[...], preferred_element_type=f32)
        mixed = (coef_a * current.astype(f32) + product) * inverse
        mid[...] = mixed.astype(bf16).reshape(PLANE, BAND, WIDE)

        def turn_mid(b, carry):
            turn(mid, b)
            return carry

        lax.fori_loop(0, ROWS // TILE, turn_mid, 0)
        gram_sum(mid, 1)
        gram[...] = total[...].astype(bf16)
        polynomial()

        rms = jnp.sqrt(squares / (D * HW))
        high = rms.astype(bf16).astype(f32)
        low = rms - high
        lane = lax.broadcasted_iota(jnp.int32, (2 * TILE, WIDE), 1)

        def give(peer):
            return pltpu.make_async_remote_copy(
                src_ref=done.at[peer], dst_ref=back.at[mine], send_sem=send_b, recv_sem=recv_b.at[mine // 4],
                device_id=(peer * 2 + core, y), device_id_type=MESH,
            )

        def finish(i, carry):
            pair = (x // 2 + 1 + i) % 2
            at = pl.ds(pair * 2 * bands_per, 2 * bands_per)
            current = mid[at].reshape(2 * TILE, WIDE)
            product = jnp.dot(current, poly[...], preferred_element_type=f32)
            mixed = (coef_a * current.astype(f32) + product) * math.sqrt(max(D, HW))
            mixed = jnp.where(lane == HW, high, jnp.where(lane == HW + 1, low, mixed))
            done[at] = mixed.astype(bf16).reshape(2 * bands_per, BAND, WIDE)
            for k in range(16):
                for h in range(2):
                    peer = (pair * 2 + h) * 16 + (z + 16 + around(k)) % 16
                    if k:
                        give(peer).start()
                    else:
                        @pl.when(peer != place)
                        def _():
                            give(peer).start()
            return carry

        lax.fori_loop(0, 2, finish, 0)
        pltpu.make_async_copy(done.at[place], back.at[mine], recv_b.at[mine // 4]).start()

    for i in range(3):
        t, at = tile_at(i)
        four = back.at[pl.ds(4 * t, 4)]
        pltpu.make_async_copy(four, four, recv_b.at[t]).wait()
        tile = back[pl.ds(4 * t, 4)].reshape(4 * BAND, WIDE)
        to_y[:, at, :] = permuted(regroup, tile).reshape(4, BAND, WIDE)
        for step in range(1, N_TENSOR):
            y_copy(to_y, land, step, i, send_z, recv_z).start()

    own = pltpu.make_async_copy(to_y.at[y], land.at[y], local_z)
    own.start()

    index_m = lax.broadcasted_iota(jnp.int32, (MATS, MATS), 0)
    index_n = lax.broadcasted_iota(jnp.int32, (MATS, MATS), 1)
    owners = owner_ref[...].astype(f32)
    owner = jnp.sum(jnp.where(index_m == index_n, owners, 0.0), axis=1, keepdims=True)
    rank = jnp.sum(jnp.where((owner == owners) & (index_n < index_m), 1.0, 0.0), axis=1, keepdims=True)
    owned = owner == dp.astype(f32)

    @pl.when(works)
    def _():
        pltpu.make_async_copy(done.at[pl.ds(0, PLANE - 1)], done.at[pl.ds(0, PLANE - 1)], send_b).wait()

    for i in range(3):
        for k in range(4):
            @pl.when(jnp.logical_not(stays(i, k)))
            def _():
                band_copy(i, k).wait_send()

        for step in range(1, N_TENSOR):
            y_copy(staged, from_y, step, i, send_y, recv_y).wait_send()
    own.wait()
    for i in range(3):
        for step in range(1, N_TENSOR):
            y_copy(to_y, land, step, i, send_z, recv_z).wait()

    to_row = one_hot(MATS * SUB, lambda o: (o % MATS) * SUB + o // MATS)
    by_row = permuted(to_row, land[...].reshape(MATS * SUB, WIDE))
    update_out[...] = jnp.concatenate([by_row[MATS * r:MATS * (r + 1), :HW] for r in range(SUB)], axis=1)
    tail = by_row[:MATS, WIDE - 128:].astype(f32)
    lane = lax.broadcasted_iota(jnp.int32, (MATS, 128), 1) - (HW - (WIDE - 128))
    matrix_rms = jnp.sum(jnp.where((lane == 0) | (lane == 1), tail, 0.0), axis=1, keepdims=True)
    slot = lax.broadcasted_iota(jnp.int32, (MATS, CAP), 1).astype(f32)
    rms_out[...] = jnp.sum(jnp.where(owned & (rank == slot), matrix_rms, 0.0), axis=0, keepdims=True)


def on_device(grad, momentum, owner):
    dma = pltpu.SemaphoreType.DMA
    band = (BAND, WIDE)
    by_y = (N_TENSOR, PER_Y * SUB, WIDE)
    vmem = pl.BlockSpec(memory_space=pltpu.VMEM)
    return pl.pallas_call(
        kernel,
        out_shape=(
            jax.ShapeDtypeStruct(momentum.shape, f32),
            jax.ShapeDtypeStruct(grad.shape, bf16),
            jax.ShapeDtypeStruct((1, CAP), f32),
        ),
        in_specs=[vmem] * 3,
        out_specs=[vmem] * 3,
        scratch_shapes=[
            pltpu.VMEM(by_y, bf16),
            pltpu.VMEM(by_y, bf16),
            pltpu.VMEM((PER_Y,) + band, bf16),
            pltpu.VMEM((PLANE,) + band, bf16),
            pltpu.VMEM((WIDE, ROWS), bf16),
            pltpu.VMEM((PLANE,) + band, bf16),
            pltpu.VMEM((PLANE,) + band, bf16),
            pltpu.VMEM((WIDE, WIDE), f32),
            pltpu.VMEM((2, WIDE // TILE, WIDE, TILE), bf16),
            pltpu.VMEM((2, WIDE // TILE, WIDE, TILE), bf16),
            pltpu.VMEM((WIDE, WIDE), bf16),
            pltpu.VMEM((WIDE, WIDE), bf16),
            pltpu.VMEM((PER_Y,) + band, bf16),
            pltpu.VMEM(by_y, bf16),
            pltpu.VMEM(by_y, bf16),
            dma((3, 3)), dma((3, 3)), dma((3, 4)), dma((4,)), dma((2, 3)), dma((2, 3)), dma, dma((3,)),
            dma((3, 3)), dma((3, 3)), dma, dma,
        ],
        compiler_params=pltpu.CompilerParams(
            collective_id=0, has_side_effects=True, vmem_limit_bytes=40 * 1024 * 1024
        ),
    )(grad, momentum, owner.reshape(1, MATS))


def solution(mesh):
    return jax.shard_map(
        on_device,
        mesh=mesh,
        in_specs=(P(None, ("dp", "tensor")), P(None, ("dp", "tensor")), P()),
        out_specs=(P(None, ("dp", "tensor")), P(None, ("dp", "tensor")), P("dp", None)),
        check_vma=False,
    )
```

```python
import math

import jax
import jax.numpy as jnp
from jax import lax
from jax.experimental import pallas as pl
from jax.experimental.pallas import tpu as pltpu
from jax.sharding import PartitionSpec as P

HW = 704
WIDE = 768
D = 2048
MATS = 48
CAP = 2
N_DP = 128
N_TENSOR = 4
SUB = 4
PLANE = N_DP // 2
PER_Y = MATS // N_TENSOR
BAND = SUB * N_TENSOR
ROWS = PLANE * BAND
TILE = 256

beta_decay = 0.95
coef_a = 3.4445
coef_b = -4.775
coef_c = 2.0315
epsilon = 1e-07

MESH = pl.DeviceIdType.MESH
f32, bf16 = jnp.float32, jnp.bfloat16


def home(t, k):
    return (k + 4 - t) % 4 * 16 + 4 * k + t


def around(i):
    return (i + 1) // 2 if i % 2 else -(i // 2)


def one_hot(size, source):
    out_row = lax.broadcasted_iota(jnp.int32, (size, size), 0)
    in_row = lax.broadcasted_iota(jnp.int32, (size, size), 1)
    return (in_row == source(out_row)).astype(f32).astype(bf16)


def permuted(matrix, value):
    return jnp.dot(matrix, value, preferred_element_type=f32).astype(bf16)


def kernel(
    grad_ref, momentum_ref, owner_ref, momentum_out, update_out, rms_out,
    staged, from_y, bands, rows, turned, mid, done, total, half, other, gram, poly, back, to_y, land,
    grad_in, momentum_in, owner_in,
    send_y, recv_y, send_p, recv_p, send_g, recv_g, send_b, recv_b, send_z, recv_z, local_y, local_z, loads,
):
    dp, y = lax.axis_index("dp"), lax.axis_index("tensor")
    core, place = dp % 2, dp // 2
    x, z = place // 16, place % 16
    wave, spot = z % 4, z // 4
    mine = 4 * wave + spot
    works = (wave < 3) & ((spot + 4 - wave) % 4 == x)
    bands_per = TILE // BAND

    fetches = [
        pltpu.make_async_copy(src, dst, loads.at[n])
        for n, (src, dst) in enumerate(((grad_ref, grad_in), (momentum_ref, momentum_in), (owner_ref, owner_in)))
    ]
    for fetch in fetches:
        fetch.start()

    barrier = pltpu.get_barrier_semaphore()
    for step in range(1, N_TENSOR):
        pl.semaphore_signal(barrier, inc=1, device_id=(dp, (y + step) % N_TENSOR), device_id_type=MESH)

    @pl.when(works)
    def _():
        pl.semaphore_signal(barrier, inc=1, device_id=(dp + 1 - 2 * core, y), device_id_type=MESH)

        def greet(step, carry):
            peer = (place + step) % PLANE
            pl.semaphore_signal(barrier, inc=1, device_id=(peer * 2 + core, y), device_id_type=MESH)
            return carry

        lax.fori_loop(1, PLANE, greet, 0)

    @pl.when(jnp.logical_not(works))
    def _():
        for j in range(PER_Y):
            pl.semaphore_signal(barrier, inc=1, device_id=(home(j // 4, j % 4) * 2 + core, y), device_id_type=MESH)

    for fetch in fetches:
        fetch.wait()

    grad = grad_in[...].astype(f32)
    new_momentum = beta_decay * momentum_in[...] + grad
    momentum_out[...] = new_momentum
    nesterov = (grad + beta_decay * new_momentum).astype(bf16)
    edge = jnp.zeros((MATS, WIDE - HW), bf16)
    by_row = jnp.concatenate(
        [jnp.concatenate([nesterov[:, HW * r:HW * (r + 1)], edge], axis=1) for r in range(SUB)], axis=0
    )
    to_matrix = one_hot(MATS * SUB, lambda o: (o % SUB) * MATS + o // SUB)
    staged[...] = permuted(to_matrix, by_row).reshape(N_TENSOR, PER_Y * SUB, WIDE)

    @pl.when(works)
    def _():
        pl.semaphore_wait(barrier, N_TENSOR - 1 + 1 + PLANE - 1)

    @pl.when(jnp.logical_not(works))
    def _():
        pl.semaphore_wait(barrier, N_TENSOR - 1 + PER_Y)

    def wave_rows(t):
        return pl.ds(t * BAND, BAND)

    def y_copy(src, dst, step, t, sends, recvs):
        peer = (y + step) % N_TENSOR
        return pltpu.make_async_remote_copy(
            src_ref=src.at[peer, wave_rows(t)], dst_ref=dst.at[y, wave_rows(t)],
            send_sem=sends.at[step - 1, t], recv_sem=recvs.at[step - 1, t],
            device_id=(dp, peer), device_id_type=MESH,
        )

    own = pltpu.make_async_copy(staged.at[y], from_y.at[y], local_y)
    own.start()
    for i in range(3):
        for step in range(1, N_TENSOR):
            y_copy(staged, from_y, step, i, send_y, recv_y).start()
    own.wait()

    def band_copy(t, n):
        k = (spot + (2, 1, 3, 0)[n]) % 4
        return pltpu.make_async_remote_copy(
            src_ref=bands.at[4 * t + k], dst_ref=rows.at[place], send_sem=send_p.at[t, n], recv_sem=recv_p.at[x],
            device_id=(home(t, k) * 2 + core, y), device_id_type=MESH,
        )

    def unless_mine(t, n, act):
        if n < 3:
            act()
        else:
            pl.when(jnp.logical_not(works & (wave == t)))(act)

    regroup = one_hot(4 * BAND, lambda o: (o // SUB % 4) * BAND + (o // BAND) * SUB + o % SUB)
    for t in range(3):
        for step in range(1, N_TENSOR):
            y_copy(staged, from_y, step, t, send_y, recv_y).wait_recv()
        tile = from_y[:, wave_rows(t), :].reshape(4 * BAND, WIDE)
        bands[pl.ds(4 * t, 4)] = permuted(regroup, tile).reshape(4, BAND, WIDE)
        if t:
            for n in range(4):
                unless_mine(t - 1, n, lambda: band_copy(t - 1, n).wait_send())
        for n in range(4):
            unless_mine(t, n, lambda: band_copy(t, n).start())

    @pl.when(works)
    def _():
        pltpu.make_async_copy(bands.at[mine], rows.at[place], recv_p.at[x]).start()

        def turn(ref, b):
            at = pl.multiple_of(b * TILE, TILE)
            turned[:, pl.ds(at, TILE)] = ref[pl.ds(b * bands_per, bands_per)].reshape(TILE, WIDE).T

        def upper(c):
            return slice(0, (c + 1) * TILE), slice(c * TILE, (c + 1) * TILE)

        def swap(slot, c):
            over = pl.ds(0, (c + 1) * TILE)
            return pltpu.make_async_remote_copy(
                src_ref=half.at[slot, c, over], dst_ref=other.at[slot, c, over],
                send_sem=send_g.at[slot, c], recv_sem=recv_g.at[slot, c],
                device_id=(dp + 1 - 2 * core, y), device_id_type=MESH,
            )

        def gram_sum(ref, slot):
            for c in (2, 1, 0):
                over, across = upper(c)
                right = ref[:, :, across].reshape(ROWS, TILE)
                half[slot, c, over] = jnp.dot(turned[over], right, preferred_element_type=f32).astype(bf16)
                swap(slot, c).start()
            for c in (2, 1, 0):
                swap(slot, c).wait()
                over, across = upper(c)
                total[over, across] = half[slot, c, over].astype(f32) + other[slot, c, over].astype(f32)

        def set_gram(scale):
            for c in range(WIDE // TILE):
                over, across = upper(c)
                block = (total[over, across] * scale * scale).astype(bf16)
                gram[over, across] = block
                for r in range(c):
                    gram[across, r * TILE:(r + 1) * TILE] = block[r * TILE:(r + 1) * TILE].T

        def polynomial():
            current = gram[...]
            square = jnp.dot(current, current, preferred_element_type=f32)
            poly[...] = (coef_b * current.astype(f32) + coef_c * square).astype(bf16)

        def arrive(i, carry):
            b = (x + i) % 4
            column = rows.at[pl.ds(b * bands_per, bands_per)]
            pltpu.make_async_copy(column, column, recv_p.at[b]).wait()
            turn(rows, b)
            return carry

        lax.fori_loop(0, ROWS // TILE, arrive, 0)
        gram_sum(rows, 0)
        diagonal = lax.broadcasted_iota(jnp.int32, (TILE, TILE), 0) == lax.broadcasted_iota(jnp.int32, (TILE, TILE), 1)
        on_diagonal = sum(
            jnp.where(diagonal, total[c * TILE:(c + 1) * TILE, c * TILE:(c + 1) * TILE], 0.0) for c in range(WIDE // TILE)
        )
        squares = jnp.sum(jnp.sum(on_diagonal, axis=1, keepdims=True), axis=0, keepdims=True)
        inverse = 1.0 / (jnp.sqrt(squares) + epsilon)
        set_gram(inverse)
        polynomial()

        for b in range(ROWS // TILE):
            at = slice(b * bands_per, (b + 1) * bands_per)
            current = rows[at].reshape(TILE, WIDE)
            product = jnp.dot(current, poly[...], preferred_element_type=f32)
            mixed = ((coef_a * current.astype(f32) + product) * inverse).astype(bf16)
            mid[at] = mixed.reshape(bands_per, BAND, WIDE)
            turned[:, b * TILE:(b + 1) * TILE] = mixed.T

        gram_sum(mid, 1)
        set_gram(1.0)
        polynomial()

        rms = jnp.sqrt(squares / (D * HW))
        high = rms.astype(bf16).astype(f32)
        low = rms - high
        lane = lax.broadcasted_iota(jnp.int32, (2 * TILE, WIDE), 1)

        def give(peer):
            return pltpu.make_async_remote_copy(
                src_ref=done.at[peer], dst_ref=back.at[mine], send_sem=send_b, recv_sem=recv_b.at[wave],
                device_id=(peer * 2 + core, y), device_id_type=MESH,
            )

        def finish(i, carry):
            pair = (x // 2 + 1 + i) % 2
            at = pl.ds(pair * 2 * bands_per, 2 * bands_per)
            current = mid[at].reshape(2 * TILE, WIDE)
            product = jnp.dot(current, poly[...], preferred_element_type=f32)
            mixed = (coef_a * current.astype(f32) + product) * math.sqrt(max(D, HW))
            mixed = jnp.where(lane == HW, high, jnp.where(lane == HW + 1, low, mixed))
            done[at] = mixed.astype(bf16).reshape(2 * bands_per, BAND, WIDE)
            for k in range(16):
                for h in range(2):
                    peer = (pair * 2 + h) * 16 + (z + 16 + around(k)) % 16
                    if k:
                        give(peer).start()
                    else:
                        @pl.when(peer != place)
                        def _():
                            give(peer).start()
            return carry

        lax.fori_loop(0, 2, finish, 0)
        pltpu.make_async_copy(done.at[place], back.at[mine], recv_b.at[wave]).start()

    for t in range(3):
        four = back.at[pl.ds(4 * t, 4)]
        pltpu.make_async_copy(four, four, recv_b.at[t]).wait()
        tile = back[pl.ds(4 * t, 4)].reshape(4 * BAND, WIDE)
        to_y[:, wave_rows(t), :] = permuted(regroup, tile).reshape(4, BAND, WIDE)
        for step in range(1, N_TENSOR):
            y_copy(to_y, land, step, t, send_z, recv_z).start()

    own = pltpu.make_async_copy(to_y.at[y], land.at[y], local_z)
    own.start()

    index_m = lax.broadcasted_iota(jnp.int32, (MATS, MATS), 0)
    index_n = lax.broadcasted_iota(jnp.int32, (MATS, MATS), 1)
    owners = owner_in[...].astype(f32)
    owner = jnp.sum(jnp.where(index_m == index_n, owners, 0.0), axis=1, keepdims=True)
    rank = jnp.sum(jnp.where((owner == owners) & (index_n < index_m), 1.0, 0.0), axis=1, keepdims=True)
    owned = owner == dp.astype(f32)

    @pl.when(works)
    def _():
        pltpu.make_async_copy(done.at[pl.ds(0, PLANE - 1)], done.at[pl.ds(0, PLANE - 1)], send_b).wait()

    for i in range(3):
        if i == 2:
            for n in range(4):
                unless_mine(i, n, lambda: band_copy(i, n).wait_send())

        for step in range(1, N_TENSOR):
            y_copy(staged, from_y, step, i, send_y, recv_y).wait_send()
    own.wait()
    for i in range(3):
        for step in range(1, N_TENSOR):
            y_copy(to_y, land, step, i, send_z, recv_z).wait()

    to_row = one_hot(MATS * SUB, lambda o: (o % MATS) * SUB + o // MATS)
    by_row = permuted(to_row, land[...].reshape(MATS * SUB, WIDE))
    update_out[...] = jnp.concatenate([by_row[MATS * r:MATS * (r + 1), :HW] for r in range(SUB)], axis=1)
    tail = by_row[:MATS, WIDE - 128:].astype(f32)
    lane = lax.broadcasted_iota(jnp.int32, (MATS, 128), 1) - (HW - (WIDE - 128))
    matrix_rms = jnp.sum(jnp.where((lane == 0) | (lane == 1), tail, 0.0), axis=1, keepdims=True)
    slot = lax.broadcasted_iota(jnp.int32, (MATS, CAP), 1).astype(f32)
    rms_out[...] = jnp.sum(jnp.where(owned & (rank == slot), matrix_rms, 0.0), axis=0, keepdims=True)


def on_device(grad, momentum, owner):
    dma = pltpu.SemaphoreType.DMA
    band = (BAND, WIDE)
    by_y = (N_TENSOR, PER_Y * SUB, WIDE)
    vmem = pl.BlockSpec(memory_space=pltpu.VMEM)
    return pl.pallas_call(
        kernel,
        out_shape=(
            jax.ShapeDtypeStruct(momentum.shape, f32),
            jax.ShapeDtypeStruct(grad.shape, bf16),
            jax.ShapeDtypeStruct((1, CAP), f32),
        ),
        in_specs=[pl.BlockSpec(memory_space=pltpu.HBM)] * 3,
        out_specs=[vmem] * 3,
        scratch_shapes=[
            pltpu.VMEM(by_y, bf16),
            pltpu.VMEM(by_y, bf16),
            pltpu.VMEM((PER_Y,) + band, bf16),
            pltpu.VMEM((PLANE,) + band, bf16),
            pltpu.VMEM((WIDE, ROWS), bf16),
            pltpu.VMEM((PLANE,) + band, bf16),
            pltpu.VMEM((PLANE,) + band, bf16),
            pltpu.VMEM((WIDE, WIDE), f32),
            pltpu.VMEM((2, WIDE // TILE, WIDE, TILE), bf16),
            pltpu.VMEM((2, WIDE // TILE, WIDE, TILE), bf16),
            pltpu.VMEM((WIDE, WIDE), bf16),
            pltpu.VMEM((WIDE, WIDE), bf16),
            pltpu.VMEM((PER_Y,) + band, bf16),
            pltpu.VMEM(by_y, bf16),
            pltpu.VMEM(by_y, bf16),
            pltpu.VMEM(grad.shape, bf16),
            pltpu.VMEM(momentum.shape, f32),
            pltpu.VMEM((1, MATS), jnp.int32),
            dma((3, 3)), dma((3, 3)), dma((3, 4)), dma((4,)), dma((2, 3)), dma((2, 3)), dma, dma((3,)),
            dma((3, 3)), dma((3, 3)), dma, dma, dma((3,)),
        ],
        compiler_params=pltpu.CompilerParams(
            collective_id=0, has_side_effects=True, vmem_limit_bytes=40 * 1024 * 1024
        ),
    )(*(pltpu.with_memory_space_constraint(v, pltpu.HBM) for v in (grad, momentum, owner.reshape(1, MATS))))


def solution(mesh):
    return jax.shard_map(
        on_device,
        mesh=mesh,
        in_specs=(P(None, ("dp", "tensor")), P(None, ("dp", "tensor")), P()),
        out_specs=(P(None, ("dp", "tensor")), P(None, ("dp", "tensor")), P("dp", None)),
        check_vma=False,
    )
```

```python
import math

import jax
import jax.numpy as jnp
from jax import lax
from jax.experimental import pallas as pl
from jax.experimental.pallas import tpu as pltpu
from jax.sharding import PartitionSpec as P

HW = 704
WIDE = 768
D = 2048
MATS = 48
CAP = 2
N_DP = 128
N_TENSOR = 4
SUB = 4
PLANE = N_DP // 2
PER_Y = MATS // N_TENSOR
BAND = SUB * N_TENSOR
ROWS = PLANE * BAND
TILE = 256

beta_decay = 0.95
coef_a = 3.4445
coef_b = -4.775
coef_c = 2.0315
epsilon = 1e-07

MESH = pl.DeviceIdType.MESH
f32, bf16 = jnp.float32, jnp.bfloat16


def home(j):
    return (j % 4) * 16 + (j * 4) // 3


def around(i):
    return (i + 1) // 2 if i % 2 else -(i // 2)


def one_hot(size, source):
    out_row = lax.broadcasted_iota(jnp.int32, (size, size), 0)
    in_row = lax.broadcasted_iota(jnp.int32, (size, size), 1)
    return (in_row == source(out_row)).astype(f32).astype(bf16)


def permuted(matrix, value):
    return jnp.dot(matrix, value, preferred_element_type=f32).astype(bf16)


def kernel(
    grad_ref, momentum_ref, owner_ref, momentum_out, update_out, rms_out,
    staged, from_y, bands, rows, turned, mid, done, total, half, other, gram, poly, back, to_y, land,
    grad_in, momentum_in, owner_in,
    send_y, recv_y, send_p, recv_p, send_g, recv_g, send_b, recv_b, send_z, recv_z, local_y, local_z, loads,
):
    dp, y = lax.axis_index("dp"), lax.axis_index("tensor")
    core, place = dp % 2, dp // 2
    x, z = place // 16, place % 16
    mine = (3 * z + 3) // 4
    works = ((mine * 4) // 3 == z) & (mine % 4 == x) & (mine < PER_Y)
    bands_per = TILE // BAND

    fetches = [
        pltpu.make_async_copy(src, dst, loads.at[n])
        for n, (src, dst) in enumerate(((grad_ref, grad_in), (momentum_ref, momentum_in), (owner_ref, owner_in)))
    ]
    for fetch in fetches:
        fetch.start()

    barrier = pltpu.get_barrier_semaphore()
    for step in range(1, N_TENSOR):
        pl.semaphore_signal(barrier, inc=1, device_id=(dp, (y + step) % N_TENSOR), device_id_type=MESH)

    @pl.when(works)
    def _():
        pl.semaphore_signal(barrier, inc=1, device_id=(dp + 1 - 2 * core, y), device_id_type=MESH)

        def greet(step, carry):
            column = (x + step) % 4
            for n in range(15):
                peer = column * 16 + (z + 8 + around(n)) % 16
                pl.semaphore_signal(barrier, inc=1, device_id=(peer * 2 + core, y), device_id_type=MESH)

            @pl.when(column != x)
            def _():
                pl.semaphore_signal(barrier, inc=1, device_id=((column * 16 + z) * 2 + core, y), device_id_type=MESH)

            return carry

        lax.fori_loop(1, 5, greet, 0)

    @pl.when(jnp.logical_not(works))
    def _():
        for j in range(PER_Y):
            pl.semaphore_signal(barrier, inc=1, device_id=(home(j) * 2 + core, y), device_id_type=MESH)

    for fetch in fetches:
        fetch.wait()

    grad = grad_in[...].astype(f32)
    new_momentum = beta_decay * momentum_in[...] + grad
    momentum_out[...] = new_momentum
    nesterov = (grad + beta_decay * new_momentum).astype(bf16)
    edge = jnp.zeros((MATS, WIDE - HW), bf16)
    by_row = jnp.concatenate(
        [jnp.concatenate([nesterov[:, HW * r:HW * (r + 1)], edge], axis=1) for r in range(SUB)], axis=0
    )
    to_matrix = one_hot(MATS * SUB, lambda o: (o % SUB) * MATS + o // SUB)
    staged[...] = permuted(to_matrix, by_row).reshape(N_TENSOR, PER_Y * SUB, WIDE)

    @pl.when(works)
    def _():
        pl.semaphore_wait(barrier, N_TENSOR - 1 + 1 + PLANE - 1)

    @pl.when(jnp.logical_not(works))
    def _():
        pl.semaphore_wait(barrier, N_TENSOR - 1 + PER_Y)

    def tile_at(i):
        t = (jnp.minimum(mine // 4, 2) + i) % 3
        return t, pl.ds(pl.multiple_of(t * BAND, BAND), BAND)

    def y_copy(src, dst, step, i, sends, recvs):
        peer = (y + step) % N_TENSOR
        at = tile_at(i)[1]
        return pltpu.make_async_remote_copy(
            src_ref=src.at[peer, at], dst_ref=dst.at[y, at],
            send_sem=sends.at[step - 1, i], recv_sem=recvs.at[step - 1, i],
            device_id=(dp, peer), device_id_type=MESH,
        )

    own = pltpu.make_async_copy(staged.at[y], from_y.at[y], local_y)
    own.start()
    for i in range(3):
        for step in range(1, N_TENSOR):
            y_copy(staged, from_y, step, i, send_y, recv_y).start()
    own.wait()

    def band_copy(i, k):
        j = tile_at(i)[0] * 4 + k
        return pltpu.make_async_remote_copy(
            src_ref=bands.at[j], dst_ref=rows.at[place], send_sem=send_p.at[i, k], recv_sem=recv_p.at[x],
            device_id=(home(j) * 2 + core, y), device_id_type=MESH,
        )

    def stays(i, k):
        return works & (tile_at(i)[0] * 4 + k == mine)

    regroup = one_hot(4 * BAND, lambda o: (o // SUB % 4) * BAND + (o // BAND) * SUB + o % SUB)
    for i in range(3):
        for step in range(1, N_TENSOR):
            y_copy(staged, from_y, step, i, send_y, recv_y).wait_recv()
        t, at = tile_at(i)
        tile = from_y[:, at, :].reshape(4 * BAND, WIDE)
        bands[pl.ds(4 * t, 4)] = permuted(regroup, tile).reshape(4, BAND, WIDE)
        for k in range(4):
            @pl.when(jnp.logical_not(stays(i, k)))
            def _():
                band_copy(i, k).start()

    @pl.when(works)
    def _():
        pltpu.make_async_copy(bands.at[mine], rows.at[place], recv_p.at[x]).start()

        def turn(ref, b):
            at = pl.multiple_of(b * TILE, TILE)
            turned[:, pl.ds(at, TILE)] = ref[pl.ds(b * bands_per, bands_per)].reshape(TILE, WIDE).T

        def upper(c):
            return slice(0, (c + 1) * TILE), slice(c * TILE, (c + 1) * TILE)

        def swap(slot, c):
            over = pl.ds(0, (c + 1) * TILE)
            return pltpu.make_async_remote_copy(
                src_ref=half.at[slot, c, over], dst_ref=other.at[slot, c, over],
                send_sem=send_g.at[slot, c], recv_sem=recv_g.at[slot, c],
                device_id=(dp + 1 - 2 * core, y), device_id_type=MESH,
            )

        def gram_sum(ref, slot):
            for c in (2, 1, 0):
                over, across = upper(c)
                right = ref[:, :, across].reshape(ROWS, TILE)
                half[slot, c, over] = jnp.dot(turned[over], right, preferred_element_type=f32).astype(bf16)
                swap(slot, c).start()
            for c in (2, 1, 0):
                swap(slot, c).wait()
                over, across = upper(c)
                total[over, across] = half[slot, c, over].astype(f32) + other[slot, c, over].astype(f32)

        def set_gram(scale):
            for c in range(WIDE // TILE):
                over, across = upper(c)
                block = (total[over, across] * scale * scale).astype(bf16)
                gram[over, across] = block
                for r in range(c):
                    gram[across, r * TILE:(r + 1) * TILE] = block[r * TILE:(r + 1) * TILE].T

        def polynomial():
            current = gram[...]
            square = jnp.dot(current, current, preferred_element_type=f32)
            poly[...] = (coef_b * current.astype(f32) + coef_c * square).astype(bf16)

        def arrive(i, carry):
            b = (x + i) % 4
            column = rows.at[pl.ds(b * bands_per, bands_per)]
            pltpu.make_async_copy(column, column, recv_p.at[b]).wait()
            turn(rows, b)
            return carry

        lax.fori_loop(0, ROWS // TILE, arrive, 0)
        gram_sum(rows, 0)
        diagonal = lax.broadcasted_iota(jnp.int32, (TILE, TILE), 0) == lax.broadcasted_iota(jnp.int32, (TILE, TILE), 1)
        on_diagonal = sum(
            jnp.where(diagonal, total[c * TILE:(c + 1) * TILE, c * TILE:(c + 1) * TILE], 0.0) for c in range(WIDE // TILE)
        )
        squares = jnp.sum(jnp.sum(on_diagonal, axis=1, keepdims=True), axis=0, keepdims=True)
        inverse = 1.0 / (jnp.sqrt(squares) + epsilon)
        set_gram(inverse)
        polynomial()

        for b in range(ROWS // TILE):
            at = slice(b * bands_per, (b + 1) * bands_per)
            current = rows[at].reshape(TILE, WIDE)
            product = jnp.dot(current, poly[...], preferred_element_type=f32)
            mixed = ((coef_a * current.astype(f32) + product) * inverse).astype(bf16)
            mid[at] = mixed.reshape(bands_per, BAND, WIDE)
            turned[:, b * TILE:(b + 1) * TILE] = mixed.T

        gram_sum(mid, 1)
        set_gram(1.0)
        polynomial()

        rms = jnp.sqrt(squares / (D * HW))
        high = rms.astype(bf16).astype(f32)
        low = rms - high
        lane = lax.broadcasted_iota(jnp.int32, (2 * TILE, WIDE), 1)

        def give(peer):
            return pltpu.make_async_remote_copy(
                src_ref=done.at[peer], dst_ref=back.at[mine], send_sem=send_b, recv_sem=recv_b.at[mine // 4],
                device_id=(peer * 2 + core, y), device_id_type=MESH,
            )

        def finish(i, carry):
            pair = (x // 2 + 1 + i) % 2
            at = pl.ds(pair * 2 * bands_per, 2 * bands_per)
            current = mid[at].reshape(2 * TILE, WIDE)
            product = jnp.dot(current, poly[...], preferred_element_type=f32)
            mixed = (coef_a * current.astype(f32) + product) * math.sqrt(max(D, HW))
            mixed = jnp.where(lane == HW, high, jnp.where(lane == HW + 1, low, mixed))
            done[at] = mixed.astype(bf16).reshape(2 * bands_per, BAND, WIDE)
            for k in range(16):
                for h in range(2):
                    peer = (pair * 2 + h) * 16 + (z + 16 + around(k)) % 16
                    if k:
                        give(peer).start()
                    else:
                        @pl.when(peer != place)
                        def _():
                            give(peer).start()
            return carry

        lax.fori_loop(0, 2, finish, 0)
        pltpu.make_async_copy(done.at[place], back.at[mine], recv_b.at[mine // 4]).start()

    for i in range(3):
        t, at = tile_at(i)
        four = back.at[pl.ds(4 * t, 4)]
        pltpu.make_async_copy(four, four, recv_b.at[t]).wait()
        tile = back[pl.ds(4 * t, 4)].reshape(4 * BAND, WIDE)
        to_y[:, at, :] = permuted(regroup, tile).reshape(4, BAND, WIDE)
        for step in range(1, N_TENSOR):
            y_copy(to_y, land, step, i, send_z, recv_z).start()

    own = pltpu.make_async_copy(to_y.at[y], land.at[y], local_z)
    own.start()

    index_m = lax.broadcasted_iota(jnp.int32, (MATS, MATS), 0)
    index_n = lax.broadcasted_iota(jnp.int32, (MATS, MATS), 1)
    owners = owner_in[...].astype(f32)
    owner = jnp.sum(jnp.where(index_m == index_n, owners, 0.0), axis=1, keepdims=True)
    rank = jnp.sum(jnp.where((owner == owners) & (index_n < index_m), 1.0, 0.0), axis=1, keepdims=True)
    owned = owner == dp.astype(f32)

    @pl.when(works)
    def _():
        pltpu.make_async_copy(done.at[pl.ds(0, PLANE - 1)], done.at[pl.ds(0, PLANE - 1)], send_b).wait()

    for i in range(3):
        for k in range(4):
            @pl.when(jnp.logical_not(stays(i, k)))
            def _():
                band_copy(i, k).wait_send()

        for step in range(1, N_TENSOR):
            y_copy(staged, from_y, step, i, send_y, recv_y).wait_send()
    own.wait()
    for i in range(3):
        for step in range(1, N_TENSOR):
            y_copy(to_y, land, step, i, send_z, recv_z).wait()

    to_row = one_hot(MATS * SUB, lambda o: (o % MATS) * SUB + o // MATS)
    by_row = permuted(to_row, land[...].reshape(MATS * SUB, WIDE))
    update_out[...] = jnp.concatenate([by_row[MATS * r:MATS * (r + 1), :HW] for r in range(SUB)], axis=1)
    tail = by_row[:MATS, WIDE - 128:].astype(f32)
    lane = lax.broadcasted_iota(jnp.int32, (MATS, 128), 1) - (HW - (WIDE - 128))
    matrix_rms = jnp.sum(jnp.where((lane == 0) | (lane == 1), tail, 0.0), axis=1, keepdims=True)
    slot = lax.broadcasted_iota(jnp.int32, (MATS, CAP), 1).astype(f32)
    rms_out[...] = jnp.sum(jnp.where(owned & (rank == slot), matrix_rms, 0.0), axis=0, keepdims=True)


def on_device(grad, momentum, owner):
    dma = pltpu.SemaphoreType.DMA
    band = (BAND, WIDE)
    by_y = (N_TENSOR, PER_Y * SUB, WIDE)
    vmem = pl.BlockSpec(memory_space=pltpu.VMEM)
    return pl.pallas_call(
        kernel,
        out_shape=(
            jax.ShapeDtypeStruct(momentum.shape, f32),
            jax.ShapeDtypeStruct(grad.shape, bf16),
            jax.ShapeDtypeStruct((1, CAP), f32),
        ),
        in_specs=[pl.BlockSpec(memory_space=pltpu.HBM)] * 3,
        out_specs=[vmem] * 3,
        scratch_shapes=[
            pltpu.VMEM(by_y, bf16),
            pltpu.VMEM(by_y, bf16),
            pltpu.VMEM((PER_Y,) + band, bf16),
            pltpu.VMEM((PLANE,) + band, bf16),
            pltpu.VMEM((WIDE, ROWS), bf16),
            pltpu.VMEM((PLANE,) + band, bf16),
            pltpu.VMEM((PLANE,) + band, bf16),
            pltpu.VMEM((WIDE, WIDE), f32),
            pltpu.VMEM((2, WIDE // TILE, WIDE, TILE), bf16),
            pltpu.VMEM((2, WIDE // TILE, WIDE, TILE), bf16),
            pltpu.VMEM((WIDE, WIDE), bf16),
            pltpu.VMEM((WIDE, WIDE), bf16),
            pltpu.VMEM((PER_Y,) + band, bf16),
            pltpu.VMEM(by_y, bf16),
            pltpu.VMEM(by_y, bf16),
            pltpu.VMEM(grad.shape, bf16),
            pltpu.VMEM(momentum.shape, f32),
            pltpu.VMEM((1, MATS), jnp.int32),
            dma((3, 3)), dma((3, 3)), dma((3, 4)), dma((4,)), dma((2, 3)), dma((2, 3)), dma, dma((3,)),
            dma((3, 3)), dma((3, 3)), dma, dma, dma((3,)),
        ],
        compiler_params=pltpu.CompilerParams(
            collective_id=0, has_side_effects=True, vmem_limit_bytes=40 * 1024 * 1024
        ),
    )(*(pltpu.with_memory_space_constraint(v, pltpu.HBM) for v in (grad, momentum, owner.reshape(1, MATS))))


def solution(mesh):
    return jax.shard_map(
        on_device,
        mesh=mesh,
        in_specs=(P(None, ("dp", "tensor")), P(None, ("dp", "tensor")), P()),
        out_specs=(P(None, ("dp", "tensor")), P(None, ("dp", "tensor")), P("dp", None)),
        check_vma=False,
    )
```

```python
import math

import jax
import jax.numpy as jnp
from jax import lax
from jax.experimental import pallas as pl
from jax.experimental.pallas import tpu as pltpu
from jax.sharding import PartitionSpec as P

HW = 704
WIDE = 768
D = 2048
MATS = 48
CAP = 2
N_DP = 128
N_TENSOR = 4
SUB = 4
PLANE = N_DP // 2
PER_Y = MATS // N_TENSOR
BAND = SUB * N_TENSOR
ROWS = PLANE * BAND
TILE = 256

beta_decay = 0.95
coef_a = 3.4445
coef_b = -4.775
coef_c = 2.0315
epsilon = 1e-07

MESH = pl.DeviceIdType.MESH
f32, bf16 = jnp.float32, jnp.bfloat16


def home(j):
    return (j % 4) * 16 + (j * 4) // 3


def around(i):
    return (i + 1) // 2 if i % 2 else -(i // 2)


def one_hot(size, source):
    out_row = lax.broadcasted_iota(jnp.int32, (size, size), 0)
    in_row = lax.broadcasted_iota(jnp.int32, (size, size), 1)
    return (in_row == source(out_row)).astype(f32).astype(bf16)


def permuted(matrix, value):
    return jnp.dot(matrix, value, preferred_element_type=f32).astype(bf16)


def kernel(
    grad_ref, momentum_ref, owner_ref, momentum_out, update_out, rms_out,
    staged, from_y, bands, rows, turned, mid, done, total, half, other, gram, poly, back, to_y, land,
    grad_in, momentum_in, owner_in,
    send_y, recv_y, send_p, recv_p, send_g, recv_g, send_b, recv_b, send_z, recv_z, local_y, local_z, loads,
):
    dp, y = lax.axis_index("dp"), lax.axis_index("tensor")
    core, place = dp % 2, dp // 2
    x, z = place // 16, place % 16
    mine = (3 * z + 3) // 4
    works = ((mine * 4) // 3 == z) & (mine % 4 == x) & (mine < PER_Y)
    bands_per = TILE // BAND

    fetches = [
        pltpu.make_async_copy(src, dst, loads.at[n])
        for n, (src, dst) in enumerate(((grad_ref, grad_in), (momentum_ref, momentum_in), (owner_ref, owner_in)))
    ]
    for fetch in fetches:
        fetch.start()

    barrier = pltpu.get_barrier_semaphore()
    for step in range(1, N_TENSOR):
        pl.semaphore_signal(barrier, inc=1, device_id=(dp, (y + step) % N_TENSOR), device_id_type=MESH)

    @pl.when(works)
    def _():
        pl.semaphore_signal(barrier, inc=1, device_id=(dp + 1 - 2 * core, y), device_id_type=MESH)

        def greet(step, carry):
            column = (x + step) % 4
            for n in range(15):
                peer = column * 16 + (z + 8 + around(n)) % 16
                pl.semaphore_signal(barrier, inc=1, device_id=(peer * 2 + core, y), device_id_type=MESH)

            @pl.when(column != x)
            def _():
                pl.semaphore_signal(barrier, inc=1, device_id=((column * 16 + z) * 2 + core, y), device_id_type=MESH)

            return carry

        lax.fori_loop(1, 5, greet, 0)

    @pl.when(jnp.logical_not(works))
    def _():
        for j in range(PER_Y):
            pl.semaphore_signal(barrier, inc=1, device_id=(home(j) * 2 + core, y), device_id_type=MESH)

    for fetch in fetches:
        fetch.wait()

    grad = grad_in[...].astype(f32)
    new_momentum = beta_decay * momentum_in[...] + grad
    momentum_out[...] = new_momentum
    nesterov = (grad + beta_decay * new_momentum).astype(bf16)
    edge = jnp.zeros((MATS, WIDE - HW), bf16)
    by_row = jnp.concatenate(
        [jnp.concatenate([nesterov[:, HW * r:HW * (r + 1)], edge], axis=1) for r in range(SUB)], axis=0
    )
    to_matrix = one_hot(MATS * SUB, lambda o: (o % SUB) * MATS + o // SUB)
    staged[...] = permuted(to_matrix, by_row).reshape(N_TENSOR, PER_Y * SUB, WIDE)

    @pl.when(works)
    def _():
        pl.semaphore_wait(barrier, N_TENSOR - 1 + 1 + PLANE - 1)

    @pl.when(jnp.logical_not(works))
    def _():
        pl.semaphore_wait(barrier, N_TENSOR - 1 + PER_Y)

    def tile_at(i):
        near = jnp.minimum(mine, PER_Y - 1)
        t = (near // 4 + 3 + i * jnp.where(near % 4 >= 2, 1, -1)) % 3
        return t, pl.ds(pl.multiple_of(t * BAND, BAND), BAND)

    def y_copy(src, dst, step, i, sends, recvs):
        peer = (y + step) % N_TENSOR
        at = tile_at(i)[1]
        return pltpu.make_async_remote_copy(
            src_ref=src.at[peer, at], dst_ref=dst.at[y, at],
            send_sem=sends.at[step - 1, i], recv_sem=recvs.at[step - 1, i],
            device_id=(dp, peer), device_id_type=MESH,
        )

    own = pltpu.make_async_copy(staged.at[y], from_y.at[y], local_y)
    own.start()
    for i in range(3):
        for step in range(1, N_TENSOR):
            y_copy(staged, from_y, step, i, send_y, recv_y).start()
    own.wait()

    def band_copy(i, k):
        j = tile_at(i)[0] * 4 + k
        return pltpu.make_async_remote_copy(
            src_ref=bands.at[j], dst_ref=rows.at[place], send_sem=send_p.at[i, k], recv_sem=recv_p.at[x],
            device_id=(home(j) * 2 + core, y), device_id_type=MESH,
        )

    def stays(i, k):
        return works & (tile_at(i)[0] * 4 + k == mine)

    regroup = one_hot(4 * BAND, lambda o: (o // SUB % 4) * BAND + (o // BAND) * SUB + o % SUB)
    for i in range(3):
        for step in range(1, N_TENSOR):
            y_copy(staged, from_y, step, i, send_y, recv_y).wait_recv()
        t, at = tile_at(i)
        tile = from_y[:, at, :].reshape(4 * BAND, WIDE)
        bands[pl.ds(4 * t, 4)] = permuted(regroup, tile).reshape(4, BAND, WIDE)
        for k in range(4):
            @pl.when(jnp.logical_not(stays(i, k)))
            def _():
                band_copy(i, k).start()

    @pl.when(works)
    def _():
        pltpu.make_async_copy(bands.at[mine], rows.at[place], recv_p.at[x]).start()

        def turn(ref, b):
            at = pl.multiple_of(b * TILE, TILE)
            turned[:, pl.ds(at, TILE)] = ref[pl.ds(b * bands_per, bands_per)].reshape(TILE, WIDE).T

        def upper(c):
            return slice(0, (c + 1) * TILE), slice(c * TILE, (c + 1) * TILE)

        def swap(slot, c):
            over = pl.ds(0, (c + 1) * TILE)
            return pltpu.make_async_remote_copy(
                src_ref=half.at[slot, c, over], dst_ref=other.at[slot, c, over],
                send_sem=send_g.at[slot, c], recv_sem=recv_g.at[slot, c],
                device_id=(dp + 1 - 2 * core, y), device_id_type=MESH,
            )

        def gram_sum(ref, slot):
            for c in (2, 1, 0):
                over, across = upper(c)
                right = ref[:, :, across].reshape(ROWS, TILE)
                half[slot, c, over] = jnp.dot(turned[over], right, preferred_element_type=f32).astype(bf16)
                swap(slot, c).start()
            for c in (2, 1, 0):
                swap(slot, c).wait()
                over, across = upper(c)
                total[over, across] = half[slot, c, over].astype(f32) + other[slot, c, over].astype(f32)

        def set_gram(scale):
            for c in range(WIDE // TILE):
                over, across = upper(c)
                block = (total[over, across] * scale * scale).astype(bf16)
                gram[over, across] = block
                for r in range(c):
                    gram[across, r * TILE:(r + 1) * TILE] = block[r * TILE:(r + 1) * TILE].T

        def polynomial():
            current = gram[...]
            square = jnp.dot(current, current, preferred_element_type=f32)
            poly[...] = (coef_b * current.astype(f32) + coef_c * square).astype(bf16)

        def arrive(i, carry):
            b = (x + i) % 4
            column = rows.at[pl.ds(b * bands_per, bands_per)]
            pltpu.make_async_copy(column, column, recv_p.at[b]).wait()
            turn(rows, b)
            return carry

        lax.fori_loop(0, ROWS // TILE, arrive, 0)
        gram_sum(rows, 0)
        diagonal = lax.broadcasted_iota(jnp.int32, (TILE, TILE), 0) == lax.broadcasted_iota(jnp.int32, (TILE, TILE), 1)
        on_diagonal = sum(
            jnp.where(diagonal, total[c * TILE:(c + 1) * TILE, c * TILE:(c + 1) * TILE], 0.0) for c in range(WIDE // TILE)
        )
        squares = jnp.sum(jnp.sum(on_diagonal, axis=1, keepdims=True), axis=0, keepdims=True)
        inverse = 1.0 / (jnp.sqrt(squares) + epsilon)
        set_gram(inverse)
        polynomial()

        for b in range(ROWS // TILE):
            at = slice(b * bands_per, (b + 1) * bands_per)
            current = rows[at].reshape(TILE, WIDE)
            product = jnp.dot(current, poly[...], preferred_element_type=f32)
            mixed = ((coef_a * current.astype(f32) + product) * inverse).astype(bf16)
            mid[at] = mixed.reshape(bands_per, BAND, WIDE)
            turned[:, b * TILE:(b + 1) * TILE] = mixed.T

        gram_sum(mid, 1)
        set_gram(1.0)
        polynomial()

        rms = jnp.sqrt(squares / (D * HW))
        high = rms.astype(bf16).astype(f32)
        low = rms - high
        lane = lax.broadcasted_iota(jnp.int32, (2 * TILE, WIDE), 1)

        def give(peer):
            return pltpu.make_async_remote_copy(
                src_ref=done.at[peer], dst_ref=back.at[mine], send_sem=send_b, recv_sem=recv_b.at[mine // 4],
                device_id=(peer * 2 + core, y), device_id_type=MESH,
            )

        def finish(i, carry):
            pair = (x // 2 + 1 + i) % 2
            at = pl.ds(pair * 2 * bands_per, 2 * bands_per)
            current = mid[at].reshape(2 * TILE, WIDE)
            product = jnp.dot(current, poly[...], preferred_element_type=f32)
            mixed = (coef_a * current.astype(f32) + product) * math.sqrt(max(D, HW))
            mixed = jnp.where(lane == HW, high, jnp.where(lane == HW + 1, low, mixed))
            done[at] = mixed.astype(bf16).reshape(2 * bands_per, BAND, WIDE)
            for k in reversed(range(16)):
                for h in range(2):
                    peer = (pair * 2 + h) * 16 + (z + 16 + around(k)) % 16
                    if k:
                        give(peer).start()
                    else:
                        @pl.when(peer != place)
                        def _():
                            give(peer).start()
            return carry

        lax.fori_loop(0, 2, finish, 0)
        pltpu.make_async_copy(done.at[place], back.at[mine], recv_b.at[mine // 4]).start()

    for i in (2, 1, 0):
        t, at = tile_at(i)
        four = back.at[pl.ds(4 * t, 4)]
        pltpu.make_async_copy(four, four, recv_b.at[t]).wait()
        tile = back[pl.ds(4 * t, 4)].reshape(4 * BAND, WIDE)
        to_y[:, at, :] = permuted(regroup, tile).reshape(4, BAND, WIDE)
        for step in range(1, N_TENSOR):
            y_copy(to_y, land, step, i, send_z, recv_z).start()

    own = pltpu.make_async_copy(to_y.at[y], land.at[y], local_z)
    own.start()

    index_m = lax.broadcasted_iota(jnp.int32, (MATS, MATS), 0)
    index_n = lax.broadcasted_iota(jnp.int32, (MATS, MATS), 1)
    owners = owner_in[...].astype(f32)
    owner = jnp.sum(jnp.where(index_m == index_n, owners, 0.0), axis=1, keepdims=True)
    rank = jnp.sum(jnp.where((owner == owners) & (index_n < index_m), 1.0, 0.0), axis=1, keepdims=True)
    owned = owner == dp.astype(f32)

    @pl.when(works)
    def _():
        pltpu.make_async_copy(done.at[pl.ds(0, PLANE - 1)], done.at[pl.ds(0, PLANE - 1)], send_b).wait()

    for i in range(3):
        for k in range(4):
            @pl.when(jnp.logical_not(stays(i, k)))
            def _():
                band_copy(i, k).wait_send()

        for step in range(1, N_TENSOR):
            y_copy(staged, from_y, step, i, send_y, recv_y).wait_send()
    own.wait()
    for i in range(3):
        for step in range(1, N_TENSOR):
            y_copy(to_y, land, step, i, send_z, recv_z).wait()

    to_row = one_hot(MATS * SUB, lambda o: (o % MATS) * SUB + o // MATS)
    by_row = permuted(to_row, land[...].reshape(MATS * SUB, WIDE))
    update_out[...] = jnp.concatenate([by_row[MATS * r:MATS * (r + 1), :HW] for r in range(SUB)], axis=1)
    tail = by_row[:MATS, WIDE - 128:].astype(f32)
    lane = lax.broadcasted_iota(jnp.int32, (MATS, 128), 1) - (HW - (WIDE - 128))
    matrix_rms = jnp.sum(jnp.where((lane == 0) | (lane == 1), tail, 0.0), axis=1, keepdims=True)
    slot = lax.broadcasted_iota(jnp.int32, (MATS, CAP), 1).astype(f32)
    rms_out[...] = jnp.sum(jnp.where(owned & (rank == slot), matrix_rms, 0.0), axis=0, keepdims=True)


def on_device(grad, momentum, owner):
    dma = pltpu.SemaphoreType.DMA
    band = (BAND, WIDE)
    by_y = (N_TENSOR, PER_Y * SUB, WIDE)
    vmem = pl.BlockSpec(memory_space=pltpu.VMEM)
    return pl.pallas_call(
        kernel,
        out_shape=(
            jax.ShapeDtypeStruct(momentum.shape, f32),
            jax.ShapeDtypeStruct(grad.shape, bf16),
            jax.ShapeDtypeStruct((1, CAP), f32),
        ),
        in_specs=[pl.BlockSpec(memory_space=pltpu.HBM)] * 3,
        out_specs=[vmem] * 3,
        scratch_shapes=[
            pltpu.VMEM(by_y, bf16),
            pltpu.VMEM(by_y, bf16),
            pltpu.VMEM((PER_Y,) + band, bf16),
            pltpu.VMEM((PLANE,) + band, bf16),
            pltpu.VMEM((WIDE, ROWS), bf16),
            pltpu.VMEM((PLANE,) + band, bf16),
            pltpu.VMEM((PLANE,) + band, bf16),
            pltpu.VMEM((WIDE, WIDE), f32),
            pltpu.VMEM((2, WIDE // TILE, WIDE, TILE), bf16),
            pltpu.VMEM((2, WIDE // TILE, WIDE, TILE), bf16),
            pltpu.VMEM((WIDE, WIDE), bf16),
            pltpu.VMEM((WIDE, WIDE), bf16),
            pltpu.VMEM((PER_Y,) + band, bf16),
            pltpu.VMEM(by_y, bf16),
            pltpu.VMEM(by_y, bf16),
            pltpu.VMEM(grad.shape, bf16),
            pltpu.VMEM(momentum.shape, f32),
            pltpu.VMEM((1, MATS), jnp.int32),
            dma((3, 3)), dma((3, 3)), dma((3, 4)), dma((4,)), dma((2, 3)), dma((2, 3)), dma, dma((3,)),
            dma((3, 3)), dma((3, 3)), dma, dma, dma((3,)),
        ],
        compiler_params=pltpu.CompilerParams(
            collective_id=0, has_side_effects=True, vmem_limit_bytes=40 * 1024 * 1024
        ),
    )(*(pltpu.with_memory_space_constraint(v, pltpu.HBM) for v in (grad, momentum, owner.reshape(1, MATS))))


def solution(mesh):
    return jax.shard_map(
        on_device,
        mesh=mesh,
        in_specs=(P(None, ("dp", "tensor")), P(None, ("dp", "tensor")), P()),
        out_specs=(P(None, ("dp", "tensor")), P(None, ("dp", "tensor")), P("dp", None)),
        check_vma=False,
    )
```

```python
import math

import jax
import jax.numpy as jnp
from jax import lax
from jax.experimental import pallas as pl
from jax.experimental.pallas import tpu as pltpu
from jax.sharding import PartitionSpec as P

HW = 704
WIDE = 768
D = 2048
MATS = 48
CAP = 2
N_DP = 128
N_TENSOR = 4
SUB = 4
PLANE = N_DP // 2
PER_Y = MATS // N_TENSOR
BAND = SUB * N_TENSOR
ROWS = PLANE * BAND
TILE = 256

beta_decay = 0.95
coef_a = 3.4445
coef_b = -4.775
coef_c = 2.0315
epsilon = 1e-07

MESH = pl.DeviceIdType.MESH
f32, bf16 = jnp.float32, jnp.bfloat16


def home(j):
    return (j % 4) * 16 + (j * 4) // 3


def around(i):
    return (i + 1) // 2 if i % 2 else -(i // 2)


def one_hot(size, source):
    out_row = lax.broadcasted_iota(jnp.int32, (size, size), 0)
    in_row = lax.broadcasted_iota(jnp.int32, (size, size), 1)
    return (in_row == source(out_row)).astype(f32).astype(bf16)


def permuted(matrix, value):
    return jnp.dot(matrix, value, preferred_element_type=f32).astype(bf16)


def kernel(
    grad_ref, momentum_ref, owner_ref, momentum_out, update_out, rms_out,
    staged, from_y, bands, rows, turned, mid, done, total, half, other, gram, poly, back, to_y, land,
    grad_in, momentum_in, owner_in,
    send_y, recv_y, send_p, recv_p, send_g, recv_g, send_b, recv_b, send_z, recv_z, local_y, local_z, loads,
):
    dp, y = lax.axis_index("dp"), lax.axis_index("tensor")
    core, place = dp % 2, dp // 2
    x, z = place // 16, place % 16
    slot = z * 4 + x
    mine = (3 * z + 3) // 4
    works = ((mine * 4) // 3 == z) & (mine % 4 == x) & (mine < PER_Y)
    bands_per = TILE // BAND

    fetches = [
        pltpu.make_async_copy(src, dst, loads.at[n])
        for n, (src, dst) in enumerate(((grad_ref, grad_in), (momentum_ref, momentum_in), (owner_ref, owner_in)))
    ]
    for fetch in fetches:
        fetch.start()

    barrier = pltpu.get_barrier_semaphore()
    for step in range(1, N_TENSOR):
        pl.semaphore_signal(barrier, inc=1, device_id=(dp, (y + step) % N_TENSOR), device_id_type=MESH)

    @pl.when(works)
    def _():
        pl.semaphore_signal(barrier, inc=1, device_id=(dp + 1 - 2 * core, y), device_id_type=MESH)

        def greet(step, carry):
            column = (x + step) % 4
            for n in range(15):
                peer = column * 16 + (z + 8 + around(n)) % 16
                pl.semaphore_signal(barrier, inc=1, device_id=(peer * 2 + core, y), device_id_type=MESH)

            @pl.when(column != x)
            def _():
                pl.semaphore_signal(barrier, inc=1, device_id=((column * 16 + z) * 2 + core, y), device_id_type=MESH)

            return carry

        lax.fori_loop(1, 5, greet, 0)

    @pl.when(jnp.logical_not(works))
    def _():
        for j in range(PER_Y):
            pl.semaphore_signal(barrier, inc=1, device_id=(home(j) * 2 + core, y), device_id_type=MESH)

    for fetch in fetches:
        fetch.wait()

    grad = grad_in[...].astype(f32)
    new_momentum = beta_decay * momentum_in[...] + grad
    momentum_out[...] = new_momentum
    nesterov = (grad + beta_decay * new_momentum).astype(bf16)
    edge = jnp.zeros((MATS, WIDE - HW), bf16)
    by_row = jnp.concatenate(
        [jnp.concatenate([nesterov[:, HW * r:HW * (r + 1)], edge], axis=1) for r in range(SUB)], axis=0
    )
    to_matrix = one_hot(MATS * SUB, lambda o: (o % SUB) * MATS + o // SUB)
    staged[...] = permuted(to_matrix, by_row).reshape(N_TENSOR, PER_Y * SUB, WIDE)

    @pl.when(works)
    def _():
        pl.semaphore_wait(barrier, N_TENSOR - 1 + 1 + PLANE - 1)

    @pl.when(jnp.logical_not(works))
    def _():
        pl.semaphore_wait(barrier, N_TENSOR - 1 + PER_Y)

    def tile_at(i):
        near = jnp.minimum(mine, PER_Y - 1)
        t = (near // 4 + 3 + i * jnp.where(near % 4 >= 2, 1, -1)) % 3
        return t, pl.ds(pl.multiple_of(t * BAND, BAND), BAND)

    def y_copy(src, dst, step, i, sends, recvs):
        peer = (y + step) % N_TENSOR
        at = tile_at(i)[1]
        return pltpu.make_async_remote_copy(
            src_ref=src.at[peer, at], dst_ref=dst.at[y, at],
            send_sem=sends.at[step - 1, i], recv_sem=recvs.at[step - 1, i],
            device_id=(dp, peer), device_id_type=MESH,
        )

    own = pltpu.make_async_copy(staged.at[y], from_y.at[y], local_y)
    own.start()
    for i in range(3):
        for step in range(1, N_TENSOR):
            y_copy(staged, from_y, step, i, send_y, recv_y).start()
    own.wait()

    def band_copy(i, k):
        j = tile_at(i)[0] * 4 + k
        return pltpu.make_async_remote_copy(
            src_ref=bands.at[j], dst_ref=rows.at[slot], send_sem=send_p.at[i, k], recv_sem=recv_p.at[z // 4],
            device_id=(home(j) * 2 + core, y), device_id_type=MESH,
        )

    def stays(i, k):
        return works & (tile_at(i)[0] * 4 + k == mine)

    regroup = one_hot(4 * BAND, lambda o: (o // SUB % 4) * BAND + (o // BAND) * SUB + o % SUB)
    for i in range(3):
        for step in range(1, N_TENSOR):
            y_copy(staged, from_y, step, i, send_y, recv_y).wait_recv()
        t, at = tile_at(i)
        tile = from_y[:, at, :].reshape(4 * BAND, WIDE)
        bands[pl.ds(4 * t, 4)] = permuted(regroup, tile).reshape(4, BAND, WIDE)
        for k in range(4):
            @pl.when(jnp.logical_not(stays(i, k)))
            def _():
                band_copy(i, k).start()

    @pl.when(works)
    def _():
        pltpu.make_async_copy(bands.at[mine], rows.at[slot], recv_p.at[z // 4]).start()

        def quarter(d):
            return (z // 4 + d) % 4

        def bands_of(d):
            return pl.ds(quarter(d) * bands_per, bands_per)

        def upper(c):
            return slice(0, (c + 1) * TILE), slice(c * TILE, (c + 1) * TILE)

        def swap(turn, c):
            over = pl.ds(0, (c + 1) * TILE)
            return pltpu.make_async_remote_copy(
                src_ref=half.at[turn, c, over], dst_ref=other.at[turn, c, over],
                send_sem=send_g.at[turn, c], recv_sem=recv_g.at[turn, c],
                device_id=(dp + 1 - 2 * core, y), device_id_type=MESH,
            )

        def give_half(turn, c, value):
            half[turn, c, upper(c)[0]] = value.astype(bf16)
            swap(turn, c).start()

        def gram_sum(turn):
            for c in (2, 1, 0):
                swap(turn, c).wait()
                over, across = upper(c)
                total[over, across] = half[turn, c, over].astype(f32) + other[turn, c, over].astype(f32)

        def set_gram(scale):
            for c in range(WIDE // TILE):
                over, across = upper(c)
                block = (total[over, across] * scale * scale).astype(bf16)
                gram[over, across] = block
                for r in range(c):
                    gram[across, r * TILE:(r + 1) * TILE] = block[r * TILE:(r + 1) * TILE].T

        def polynomial():
            current = gram[...]
            square = jnp.dot(current, current, preferred_element_type=f32)
            poly[...] = (coef_b * current.astype(f32) + coef_c * square).astype(bf16)

        for ds in ((0,), (1, 3), (2,)):
            for d in ds:
                part = rows.at[bands_of(d)]
                pltpu.make_async_copy(part, part, recv_p.at[quarter(d)]).wait()
                at = pl.multiple_of(quarter(d) * TILE, TILE)
                turned[:, pl.ds(at, TILE)] = rows[bands_of(d)].reshape(TILE, WIDE).T
            for c in (2, 1, 0):
                over, across = upper(c)
                value = total[over, across] if ds[0] else 0.0
                for d in ds:
                    at = pl.multiple_of(quarter(d) * TILE, TILE)
                    right = rows[bands_of(d), :, across].reshape(TILE, TILE)
                    value += jnp.dot(turned[over, pl.ds(at, TILE)], right, preferred_element_type=f32)
                if ds[0] == 2:
                    give_half(0, c, value)
                else:
                    total[over, across] = value

        gram_sum(0)
        diagonal = lax.broadcasted_iota(jnp.int32, (TILE, TILE), 0) == lax.broadcasted_iota(jnp.int32, (TILE, TILE), 1)
        on_diagonal = sum(
            jnp.where(diagonal, total[c * TILE:(c + 1) * TILE, c * TILE:(c + 1) * TILE], 0.0) for c in range(WIDE // TILE)
        )
        squares = jnp.sum(jnp.sum(on_diagonal, axis=1, keepdims=True), axis=0, keepdims=True)
        inverse = 1.0 / (jnp.sqrt(squares) + epsilon)
        set_gram(inverse)
        polynomial()

        for b in range(ROWS // TILE):
            at = slice(b * bands_per, (b + 1) * bands_per)
            current = rows[at].reshape(TILE, WIDE)
            product = jnp.dot(current, poly[...], preferred_element_type=f32)
            mixed = ((coef_a * current.astype(f32) + product) * inverse).astype(bf16)
            mid[at] = mixed.reshape(bands_per, BAND, WIDE)
            turned[:, b * TILE:(b + 1) * TILE] = mixed.T

        for c in (2, 1, 0):
            over, across = upper(c)
            right = mid[:, :, across].reshape(ROWS, TILE)
            give_half(1, c, jnp.dot(turned[over], right, preferred_element_type=f32))
        gram_sum(1)
        set_gram(1.0)
        polynomial()

        rms = jnp.sqrt(squares / (D * HW))
        high = rms.astype(bf16).astype(f32)
        low = rms - high
        def give(peer_x, peer_z):
            return pltpu.make_async_remote_copy(
                src_ref=done.at[peer_z * 4 + peer_x], dst_ref=back.at[mine], send_sem=send_b, recv_sem=recv_b.at[mine // 4],
                device_id=((peer_x * 16 + peer_z) * 2 + core, y), device_id_type=MESH,
            )

        far = [(2, r) for r in (1, 2, 0, 3)]
        sides = [pair for n in range(4) for pair in ((1, 3 - n), (3, n))]
        own = [(0, (z + n) % 4) for n in (2, 3, 1, 0)]
        for ds, peers in (((2,), far), ((1, 3), sides), ((0,), own)):
            current = jnp.concatenate([mid[bands_of(d)].reshape(TILE, WIDE) for d in ds], axis=0)
            lane = lax.broadcasted_iota(jnp.int32, current.shape, 1)
            product = jnp.dot(current, poly[...], preferred_element_type=f32)
            mixed = (coef_a * current.astype(f32) + product) * math.sqrt(max(D, HW))
            mixed = jnp.where(lane == HW, high, jnp.where(lane == HW + 1, low, mixed)).astype(bf16)
            for n, d in enumerate(ds):
                done[bands_of(d)] = mixed[n * TILE:(n + 1) * TILE].reshape(bands_per, BAND, WIDE)
            for n, (d, r) in enumerate(peers):
                for h in (2, 1, 3, 0):
                    if d or n < 3 or h:
                        give((x + h) % 4, quarter(d) * 4 + r).start()

        pltpu.make_async_copy(done.at[slot], back.at[mine], recv_b.at[mine // 4]).start()

    for i in (2, 1, 0):
        t, at = tile_at(i)
        four = back.at[pl.ds(4 * t, 4)]
        pltpu.make_async_copy(four, four, recv_b.at[t]).wait()
        tile = back[pl.ds(4 * t, 4)].reshape(4 * BAND, WIDE)
        to_y[:, at, :] = permuted(regroup, tile).reshape(4, BAND, WIDE)
        for step in range(1, N_TENSOR):
            y_copy(to_y, land, step, i, send_z, recv_z).start()

    own = pltpu.make_async_copy(to_y.at[y], land.at[y], local_z)
    own.start()

    index_m = lax.broadcasted_iota(jnp.int32, (MATS, MATS), 0)
    index_n = lax.broadcasted_iota(jnp.int32, (MATS, MATS), 1)
    owners = owner_in[...].astype(f32)
    owner = jnp.sum(jnp.where(index_m == index_n, owners, 0.0), axis=1, keepdims=True)
    rank = jnp.sum(jnp.where((owner == owners) & (index_n < index_m), 1.0, 0.0), axis=1, keepdims=True)
    owned = owner == dp.astype(f32)

    @pl.when(works)
    def _():
        pltpu.make_async_copy(done.at[pl.ds(0, PLANE - 1)], done.at[pl.ds(0, PLANE - 1)], send_b).wait()

    for i in range(3):
        for k in range(4):
            @pl.when(jnp.logical_not(stays(i, k)))
            def _():
                band_copy(i, k).wait_send()

        for step in range(1, N_TENSOR):
            y_copy(staged, from_y, step, i, send_y, recv_y).wait_send()
    own.wait()
    for i in range(3):
        for step in range(1, N_TENSOR):
            y_copy(to_y, land, step, i, send_z, recv_z).wait()

    to_row = one_hot(MATS * SUB, lambda o: (o % MATS) * SUB + o // MATS)
    by_row = permuted(to_row, land[...].reshape(MATS * SUB, WIDE))
    update_out[...] = jnp.concatenate([by_row[MATS * r:MATS * (r + 1), :HW] for r in range(SUB)], axis=1)
    tail = by_row[:MATS, WIDE - 128:].astype(f32)
    lane = lax.broadcasted_iota(jnp.int32, (MATS, 128), 1) - (HW - (WIDE - 128))
    matrix_rms = jnp.sum(jnp.where((lane == 0) | (lane == 1), tail, 0.0), axis=1, keepdims=True)
    ranks = lax.broadcasted_iota(jnp.int32, (MATS, CAP), 1).astype(f32)
    rms_out[...] = jnp.sum(jnp.where(owned & (rank == ranks), matrix_rms, 0.0), axis=0, keepdims=True)


def on_device(grad, momentum, owner):
    dma = pltpu.SemaphoreType.DMA
    band = (BAND, WIDE)
    by_y = (N_TENSOR, PER_Y * SUB, WIDE)
    vmem = pl.BlockSpec(memory_space=pltpu.VMEM)
    return pl.pallas_call(
        kernel,
        out_shape=(
            jax.ShapeDtypeStruct(momentum.shape, f32),
            jax.ShapeDtypeStruct(grad.shape, bf16),
            jax.ShapeDtypeStruct((1, CAP), f32),
        ),
        in_specs=[pl.BlockSpec(memory_space=pltpu.HBM)] * 3,
        out_specs=[vmem] * 3,
        scratch_shapes=[
            pltpu.VMEM(by_y, bf16),
            pltpu.VMEM(by_y, bf16),
            pltpu.VMEM((PER_Y,) + band, bf16),
            pltpu.VMEM((PLANE,) + band, bf16),
            pltpu.VMEM((WIDE, ROWS), bf16),
            pltpu.VMEM((PLANE,) + band, bf16),
            pltpu.VMEM((PLANE,) + band, bf16),
            pltpu.VMEM((WIDE, WIDE), f32),
            pltpu.VMEM((2, WIDE // TILE, WIDE, TILE), bf16),
            pltpu.VMEM((2, WIDE // TILE, WIDE, TILE), bf16),
            pltpu.VMEM((WIDE, WIDE), bf16),
            pltpu.VMEM((WIDE, WIDE), bf16),
            pltpu.VMEM((PER_Y,) + band, bf16),
            pltpu.VMEM(by_y, bf16),
            pltpu.VMEM(by_y, bf16),
            pltpu.VMEM(grad.shape, bf16),
            pltpu.VMEM(momentum.shape, f32),
            pltpu.VMEM((1, MATS), jnp.int32),
            dma((3, 3)), dma((3, 3)), dma((3, 4)), dma((4,)), dma((2, 3)), dma((2, 3)), dma, dma((3,)),
            dma((3, 3)), dma((3, 3)), dma, dma, dma((3,)),
        ],
        compiler_params=pltpu.CompilerParams(
            collective_id=0, has_side_effects=True, vmem_limit_bytes=40 * 1024 * 1024
        ),
    )(*(pltpu.with_memory_space_constraint(v, pltpu.HBM) for v in (grad, momentum, owner.reshape(1, MATS))))


def solution(mesh):
    return jax.shard_map(
        on_device,
        mesh=mesh,
        in_specs=(P(None, ("dp", "tensor")), P(None, ("dp", "tensor")), P()),
        out_specs=(P(None, ("dp", "tensor")), P(None, ("dp", "tensor")), P("dp", None)),
        check_vma=False,
    )
```

```python
import math

import jax
import jax.numpy as jnp
from jax import lax
from jax.experimental import pallas as pl
from jax.experimental.pallas import tpu as pltpu
from jax.sharding import PartitionSpec as P

HW = 704
WIDE = 768
D = 2048
MATS = 48
CAP = 2
N_DP = 128
N_TENSOR = 4
SUB = 4
PLANE = N_DP // 2
PER_Y = MATS // N_TENSOR
BAND = SUB * N_TENSOR
ROWS = PLANE * BAND
TILE = 256

beta_decay = 0.95
coef_a = 3.4445
coef_b = -4.775
coef_c = 2.0315
epsilon = 1e-07

MESH = pl.DeviceIdType.MESH
f32, bf16 = jnp.float32, jnp.bfloat16


def home(j):
    return (j % 4) * 16 + (j * 4) // 3


def around(i):
    return (i + 1) // 2 if i % 2 else -(i // 2)


def one_hot(size, source):
    out_row = lax.broadcasted_iota(jnp.int32, (size, size), 0)
    in_row = lax.broadcasted_iota(jnp.int32, (size, size), 1)
    return (in_row == source(out_row)).astype(f32).astype(bf16)


def permuted(matrix, value):
    return jnp.dot(matrix, value, preferred_element_type=f32).astype(bf16)


def kernel(
    grad_ref, momentum_ref, owner_ref, momentum_out, update_out, rms_out,
    staged, from_y, bands, rows, turned, mid, done, total, half, other, gram, poly, back, to_y, land,
    grad_in, momentum_in, owner_in,
    send_y, recv_y, send_p, recv_p, send_g, recv_g, send_b, recv_b, send_z, recv_z, local_y, local_z, loads,
):
    dp, y = lax.axis_index("dp"), lax.axis_index("tensor")
    core, place = dp % 2, dp // 2
    x, z = place // 16, place % 16
    slot = z * 4 + x
    mine = (3 * z + 3) // 4
    works = ((mine * 4) // 3 == z) & (mine % 4 == x) & (mine < PER_Y)
    bands_per = TILE // BAND

    fetches = [
        pltpu.make_async_copy(src, dst, loads.at[n])
        for n, (src, dst) in enumerate(((grad_ref, grad_in), (momentum_ref, momentum_in), (owner_ref, owner_in)))
    ]
    for fetch in fetches:
        fetch.start()

    barrier = pltpu.get_barrier_semaphore()
    for step in range(1, N_TENSOR):
        pl.semaphore_signal(barrier, inc=1, device_id=(dp, (y + step) % N_TENSOR), device_id_type=MESH)

    @pl.when(works)
    def _():
        pl.semaphore_signal(barrier, inc=1, device_id=(dp + 1 - 2 * core, y), device_id_type=MESH)

        def greet(step, carry):
            column = (x + step) % 4
            for n in range(15):
                peer = column * 16 + (z + 8 + around(n)) % 16
                pl.semaphore_signal(barrier, inc=1, device_id=(peer * 2 + core, y), device_id_type=MESH)

            @pl.when(column != x)
            def _():
                pl.semaphore_signal(barrier, inc=1, device_id=((column * 16 + z) * 2 + core, y), device_id_type=MESH)

            return carry

        lax.fori_loop(1, 5, greet, 0)

    @pl.when(jnp.logical_not(works))
    def _():
        for j in range(PER_Y):
            pl.semaphore_signal(barrier, inc=1, device_id=(home(j) * 2 + core, y), device_id_type=MESH)

    for fetch in fetches:
        fetch.wait()

    grad = grad_in[...].astype(f32)
    new_momentum = beta_decay * momentum_in[...] + grad
    momentum_out[...] = new_momentum
    nesterov = (grad + beta_decay * new_momentum).astype(bf16)
    edge = jnp.zeros((MATS, WIDE - HW), bf16)
    by_row = jnp.concatenate(
        [jnp.concatenate([nesterov[:, HW * r:HW * (r + 1)], edge], axis=1) for r in range(SUB)], axis=0
    )
    to_matrix = one_hot(MATS * SUB, lambda o: (o % SUB) * MATS + o // SUB)
    staged[...] = permuted(to_matrix, by_row).reshape(N_TENSOR, PER_Y * SUB, WIDE)

    @pl.when(works)
    def _():
        pl.semaphore_wait(barrier, N_TENSOR - 1 + 1 + PLANE - 1)

    @pl.when(jnp.logical_not(works))
    def _():
        pl.semaphore_wait(barrier, N_TENSOR - 1 + PER_Y)

    near = jnp.minimum(mine, PER_Y - 1)
    upward = near % 4 >= 2

    def tile_at(i):
        t = (near // 4 + 3 + i * jnp.where(upward, 1, -1)) % 3
        return t, pl.ds(pl.multiple_of(t * BAND, BAND), BAND)

    def y_copy(src, dst, step, i, sends, recvs):
        peer = (y + step) % N_TENSOR
        at = tile_at(i)[1]
        return pltpu.make_async_remote_copy(
            src_ref=src.at[peer, at], dst_ref=dst.at[y, at],
            send_sem=sends.at[step - 1, i], recv_sem=recvs.at[step - 1, i],
            device_id=(dp, peer), device_id_type=MESH,
        )

    own = pltpu.make_async_copy(staged.at[y], from_y.at[y], local_y)
    own.start()
    for i in range(3):
        for step in range(1, N_TENSOR):
            y_copy(staged, from_y, step, i, send_y, recv_y).start()
    own.wait()

    def matrix_at(i, n):
        k = n if i == 0 else jnp.where(upward == (i == 1), n, 3 - n)
        return tile_at(i)[0] * 4 + k

    def band_copy(i, n):
        j = matrix_at(i, n)
        return pltpu.make_async_remote_copy(
            src_ref=bands.at[j], dst_ref=rows.at[slot], send_sem=send_p.at[i, n], recv_sem=recv_p.at[z // 4],
            device_id=(home(j) * 2 + core, y), device_id_type=MESH,
        )

    def unless_mine(i, n, act):
        if i:
            act()
        else:
            pl.when(jnp.logical_not(works & (matrix_at(0, n) == mine)))(act)

    regroup = one_hot(4 * BAND, lambda o: (o // SUB % 4) * BAND + (o // BAND) * SUB + o % SUB)
    for i in range(3):
        for step in range(1, N_TENSOR):
            y_copy(staged, from_y, step, i, send_y, recv_y).wait_recv()
        t, at = tile_at(i)
        tile = from_y[:, at, :].reshape(4 * BAND, WIDE)
        bands[pl.ds(4 * t, 4)] = permuted(regroup, tile).reshape(4, BAND, WIDE)
        if i == 0:
            for n in range(4):
                unless_mine(0, n, lambda: band_copy(0, n).start())
    for n in range(4):
        for i in (1, 2):
            band_copy(i, n).start()

    @pl.when(works)
    def _():
        pltpu.make_async_copy(bands.at[mine], rows.at[slot], recv_p.at[z // 4]).start()

        def quarter(d):
            return (z // 4 + d) % 4

        def bands_of(d):
            return pl.ds(quarter(d) * bands_per, bands_per)

        def upper(c):
            return slice(0, (c + 1) * TILE), slice(c * TILE, (c + 1) * TILE)

        def swap(turn, c):
            over = pl.ds(0, (c + 1) * TILE)
            return pltpu.make_async_remote_copy(
                src_ref=half.at[turn, c, over], dst_ref=other.at[turn, c, over],
                send_sem=send_g.at[turn, c], recv_sem=recv_g.at[turn, c],
                device_id=(dp + 1 - 2 * core, y), device_id_type=MESH,
            )

        def give_half(turn, c, value):
            half[turn, c, upper(c)[0]] = value.astype(bf16)
            swap(turn, c).start()

        def gram_sum(turn):
            for c in (2, 1, 0):
                swap(turn, c).wait()
                over, across = upper(c)
                total[over, across] = half[turn, c, over].astype(f32) + other[turn, c, over].astype(f32)

        def set_gram(scale):
            for c in range(WIDE // TILE):
                over, across = upper(c)
                block = (total[over, across] * scale * scale).astype(bf16)
                gram[over, across] = block
                for r in range(c):
                    gram[across, r * TILE:(r + 1) * TILE] = block[r * TILE:(r + 1) * TILE].T

        def polynomial():
            current = gram[...]
            square = jnp.dot(current, current, preferred_element_type=f32)
            poly[...] = (coef_b * current.astype(f32) + coef_c * square).astype(bf16)

        for ds in ((0,), (1, 3), (2,)):
            for d in ds:
                part = rows.at[bands_of(d)]
                pltpu.make_async_copy(part, part, recv_p.at[quarter(d)]).wait()
                at = pl.multiple_of(quarter(d) * TILE, TILE)
                turned[:, pl.ds(at, TILE)] = rows[bands_of(d)].reshape(TILE, WIDE).T
            for c in (2, 1, 0):
                over, across = upper(c)
                value = total[over, across] if ds[0] else 0.0
                for d in ds:
                    at = pl.multiple_of(quarter(d) * TILE, TILE)
                    right = rows[bands_of(d), :, across].reshape(TILE, TILE)
                    value += jnp.dot(turned[over, pl.ds(at, TILE)], right, preferred_element_type=f32)
                if ds[0] == 2:
                    give_half(0, c, value)
                else:
                    total[over, across] = value

        gram_sum(0)
        diagonal = lax.broadcasted_iota(jnp.int32, (TILE, TILE), 0) == lax.broadcasted_iota(jnp.int32, (TILE, TILE), 1)
        on_diagonal = sum(
            jnp.where(diagonal, total[c * TILE:(c + 1) * TILE, c * TILE:(c + 1) * TILE], 0.0) for c in range(WIDE // TILE)
        )
        squares = jnp.sum(jnp.sum(on_diagonal, axis=1, keepdims=True), axis=0, keepdims=True)
        inverse = 1.0 / (jnp.sqrt(squares) + epsilon)
        set_gram(inverse)
        polynomial()

        for b in range(ROWS // TILE):
            at = slice(b * bands_per, (b + 1) * bands_per)
            current = rows[at].reshape(TILE, WIDE)
            product = jnp.dot(current, poly[...], preferred_element_type=f32)
            mixed = ((coef_a * current.astype(f32) + product) * inverse).astype(bf16)
            mid[at] = mixed.reshape(bands_per, BAND, WIDE)
            turned[:, b * TILE:(b + 1) * TILE] = mixed.T

        for c in (2, 1, 0):
            over, across = upper(c)
            right = mid[:, :, across].reshape(ROWS, TILE)
            give_half(1, c, jnp.dot(turned[over], right, preferred_element_type=f32))
        gram_sum(1)
        set_gram(1.0)
        polynomial()

        rms = jnp.sqrt(squares / (D * HW))
        high = rms.astype(bf16).astype(f32)
        low = rms - high
        def give(peer_x, peer_z):
            return pltpu.make_async_remote_copy(
                src_ref=done.at[peer_z * 4 + peer_x], dst_ref=back.at[mine], send_sem=send_b, recv_sem=recv_b.at[mine // 4],
                device_id=((peer_x * 16 + peer_z) * 2 + core, y), device_id_type=MESH,
            )

        far = [(2, r) for r in (1, 2, 0, 3)]
        sides = [pair for n in range(4) for pair in ((1, 3 - n), (3, n))]
        own = [(0, (z + n) % 4) for n in (2, 3, 1, 0)]
        for ds, peers in (((2,), far), ((1, 3), sides), ((0,), own)):
            current = jnp.concatenate([mid[bands_of(d)].reshape(TILE, WIDE) for d in ds], axis=0)
            lane = lax.broadcasted_iota(jnp.int32, current.shape, 1)
            product = jnp.dot(current, poly[...], preferred_element_type=f32)
            mixed = (coef_a * current.astype(f32) + product) * math.sqrt(max(D, HW))
            mixed = jnp.where(lane == HW, high, jnp.where(lane == HW + 1, low, mixed)).astype(bf16)
            for n, d in enumerate(ds):
                done[bands_of(d)] = mixed[n * TILE:(n + 1) * TILE].reshape(bands_per, BAND, WIDE)
            for n, (d, r) in enumerate(peers):
                for h in (2, 1, 3, 0):
                    if d or n < 3 or h:
                        give((x + h) % 4, quarter(d) * 4 + r).start()

        pltpu.make_async_copy(done.at[slot], back.at[mine], recv_b.at[mine // 4]).start()

    for i in (2, 1, 0):
        t, at = tile_at(i)
        four = back.at[pl.ds(4 * t, 4)]
        pltpu.make_async_copy(four, four, recv_b.at[t]).wait()
        tile = back[pl.ds(4 * t, 4)].reshape(4 * BAND, WIDE)
        to_y[:, at, :] = permuted(regroup, tile).reshape(4, BAND, WIDE)
        for step in range(1, N_TENSOR):
            y_copy(to_y, land, step, i, send_z, recv_z).start()

    own = pltpu.make_async_copy(to_y.at[y], land.at[y], local_z)
    own.start()

    index_m = lax.broadcasted_iota(jnp.int32, (MATS, MATS), 0)
    index_n = lax.broadcasted_iota(jnp.int32, (MATS, MATS), 1)
    owners = owner_in[...].astype(f32)
    owner = jnp.sum(jnp.where(index_m == index_n, owners, 0.0), axis=1, keepdims=True)
    rank = jnp.sum(jnp.where((owner == owners) & (index_n < index_m), 1.0, 0.0), axis=1, keepdims=True)
    owned = owner == dp.astype(f32)

    @pl.when(works)
    def _():
        pltpu.make_async_copy(done.at[pl.ds(0, PLANE - 1)], done.at[pl.ds(0, PLANE - 1)], send_b).wait()

    for i in range(3):
        for n in range(4):
            unless_mine(i, n, lambda: band_copy(i, n).wait_send())

        for step in range(1, N_TENSOR):
            y_copy(staged, from_y, step, i, send_y, recv_y).wait_send()
    own.wait()
    for i in range(3):
        for step in range(1, N_TENSOR):
            y_copy(to_y, land, step, i, send_z, recv_z).wait()

    to_row = one_hot(MATS * SUB, lambda o: (o % MATS) * SUB + o // MATS)
    by_row = permuted(to_row, land[...].reshape(MATS * SUB, WIDE))
    update_out[...] = jnp.concatenate([by_row[MATS * r:MATS * (r + 1), :HW] for r in range(SUB)], axis=1)
    tail = by_row[:MATS, WIDE - 128:].astype(f32)
    lane = lax.broadcasted_iota(jnp.int32, (MATS, 128), 1) - (HW - (WIDE - 128))
    matrix_rms = jnp.sum(jnp.where((lane == 0) | (lane == 1), tail, 0.0), axis=1, keepdims=True)
    ranks = lax.broadcasted_iota(jnp.int32, (MATS, CAP), 1).astype(f32)
    rms_out[...] = jnp.sum(jnp.where(owned & (rank == ranks), matrix_rms, 0.0), axis=0, keepdims=True)


def on_device(grad, momentum, owner):
    dma = pltpu.SemaphoreType.DMA
    band = (BAND, WIDE)
    by_y = (N_TENSOR, PER_Y * SUB, WIDE)
    vmem = pl.BlockSpec(memory_space=pltpu.VMEM)
    return pl.pallas_call(
        kernel,
        out_shape=(
            jax.ShapeDtypeStruct(momentum.shape, f32),
            jax.ShapeDtypeStruct(grad.shape, bf16),
            jax.ShapeDtypeStruct((1, CAP), f32),
        ),
        in_specs=[pl.BlockSpec(memory_space=pltpu.HBM)] * 3,
        out_specs=[vmem] * 3,
        scratch_shapes=[
            pltpu.VMEM(by_y, bf16),
            pltpu.VMEM(by_y, bf16),
            pltpu.VMEM((PER_Y,) + band, bf16),
            pltpu.VMEM((PLANE,) + band, bf16),
            pltpu.VMEM((WIDE, ROWS), bf16),
            pltpu.VMEM((PLANE,) + band, bf16),
            pltpu.VMEM((PLANE,) + band, bf16),
            pltpu.VMEM((WIDE, WIDE), f32),
            pltpu.VMEM((2, WIDE // TILE, WIDE, TILE), bf16),
            pltpu.VMEM((2, WIDE // TILE, WIDE, TILE), bf16),
            pltpu.VMEM((WIDE, WIDE), bf16),
            pltpu.VMEM((WIDE, WIDE), bf16),
            pltpu.VMEM((PER_Y,) + band, bf16),
            pltpu.VMEM(by_y, bf16),
            pltpu.VMEM(by_y, bf16),
            pltpu.VMEM(grad.shape, bf16),
            pltpu.VMEM(momentum.shape, f32),
            pltpu.VMEM((1, MATS), jnp.int32),
            dma((3, 3)), dma((3, 3)), dma((3, 4)), dma((4,)), dma((2, 3)), dma((2, 3)), dma, dma((3,)),
            dma((3, 3)), dma((3, 3)), dma, dma, dma((3,)),
        ],
        compiler_params=pltpu.CompilerParams(
            collective_id=0, has_side_effects=True, vmem_limit_bytes=40 * 1024 * 1024
        ),
    )(*(pltpu.with_memory_space_constraint(v, pltpu.HBM) for v in (grad, momentum, owner.reshape(1, MATS))))


def solution(mesh):
    return jax.shard_map(
        on_device,
        mesh=mesh,
        in_specs=(P(None, ("dp", "tensor")), P(None, ("dp", "tensor")), P()),
        out_specs=(P(None, ("dp", "tensor")), P(None, ("dp", "tensor")), P("dp", None)),
        check_vma=False,
    )
```

```python
import math

import jax
import jax.numpy as jnp
from jax import lax
from jax.experimental import pallas as pl
from jax.experimental.pallas import tpu as pltpu
from jax.sharding import PartitionSpec as P

HW = 704
WIDE = 768
D = 2048
MATS = 48
CAP = 2
N_DP = 128
N_TENSOR = 4
SUB = 4
PLANE = N_DP // 2
PER_Y = MATS // N_TENSOR
BAND = SUB * N_TENSOR
ROWS = PLANE * BAND
TILE = 256

beta_decay = 0.95
coef_a = 3.4445
coef_b = -4.775
coef_c = 2.0315
epsilon = 1e-07

MESH = pl.DeviceIdType.MESH
f32, bf16 = jnp.float32, jnp.bfloat16


def home(j):
    return (j % 4) * 16 + (j * 4) // 3


def around(i):
    return (i + 1) // 2 if i % 2 else -(i // 2)


def one_hot(size, source):
    out_row = lax.broadcasted_iota(jnp.int32, (size, size), 0)
    in_row = lax.broadcasted_iota(jnp.int32, (size, size), 1)
    return (in_row == source(out_row)).astype(f32).astype(bf16)


def permuted(matrix, value):
    return jnp.dot(matrix, value, preferred_element_type=f32).astype(bf16)


def kernel(
    grad_ref, momentum_ref, owner_ref, momentum_out, update_out, rms_out,
    staged, from_y, bands, rows, turned, mid, done, total, half, other, gram, poly, back, to_y, land,
    grad_in, momentum_in, owner_in,
    send_y, recv_y, send_p, recv_p, send_g, recv_g, send_b, recv_b, send_z, recv_z, local_y, local_z, loads,
):
    dp, y = lax.axis_index("dp"), lax.axis_index("tensor")
    core, place = dp % 2, dp // 2
    x, z = place // 16, place % 16
    slot = z * 4 + x
    mine = (3 * z + 3) // 4
    works = ((mine * 4) // 3 == z) & (mine % 4 == x) & (mine < PER_Y)
    bands_per = TILE // BAND

    fetches = [
        pltpu.make_async_copy(src, dst, loads.at[n])
        for n, (src, dst) in enumerate(((grad_ref, grad_in), (momentum_ref, momentum_in), (owner_ref, owner_in)))
    ]
    for fetch in fetches:
        fetch.start()

    barrier = pltpu.get_barrier_semaphore()
    for step in range(1, N_TENSOR):
        pl.semaphore_signal(barrier, inc=1, device_id=(dp, (y + step) % N_TENSOR), device_id_type=MESH)

    @pl.when(works)
    def _():
        pl.semaphore_signal(barrier, inc=1, device_id=(dp + 1 - 2 * core, y), device_id_type=MESH)

        def greet(step, carry):
            column = (x + step) % 4
            for n in range(15):
                peer = column * 16 + (z + 8 + around(n)) % 16
                pl.semaphore_signal(barrier, inc=1, device_id=(peer * 2 + core, y), device_id_type=MESH)

            @pl.when(column != x)
            def _():
                pl.semaphore_signal(barrier, inc=1, device_id=((column * 16 + z) * 2 + core, y), device_id_type=MESH)

            return carry

        lax.fori_loop(1, 5, greet, 0)

    @pl.when(jnp.logical_not(works))
    def _():
        for j in range(PER_Y):
            pl.semaphore_signal(barrier, inc=1, device_id=(home(j) * 2 + core, y), device_id_type=MESH)

    for fetch in fetches:
        fetch.wait()

    grad = grad_in[...].astype(f32)
    new_momentum = beta_decay * momentum_in[...] + grad
    momentum_out[...] = new_momentum
    nesterov = (grad + beta_decay * new_momentum).astype(bf16)
    edge = jnp.zeros((MATS, WIDE - HW), bf16)
    by_row = jnp.concatenate(
        [jnp.concatenate([nesterov[:, HW * r:HW * (r + 1)], edge], axis=1) for r in range(SUB)], axis=0
    )
    to_matrix = one_hot(MATS * SUB, lambda o: (o % SUB) * MATS + o // SUB)
    staged[...] = permuted(to_matrix, by_row).reshape(N_TENSOR, PER_Y * SUB, WIDE)

    @pl.when(works)
    def _():
        pl.semaphore_wait(barrier, N_TENSOR - 1 + 1 + PLANE - 1)

    @pl.when(jnp.logical_not(works))
    def _():
        pl.semaphore_wait(barrier, N_TENSOR - 1 + PER_Y)

    def tile_at(i):
        near = jnp.minimum(mine, PER_Y - 1)
        t = (near // 4 + 3 + i * jnp.where(near % 4 >= 2, 1, -1)) % 3
        return t, pl.ds(pl.multiple_of(t * BAND, BAND), BAND)

    def y_copy(src, dst, step, i, sends, recvs):
        peer = (y + step) % N_TENSOR
        at = tile_at(i)[1]
        return pltpu.make_async_remote_copy(
            src_ref=src.at[peer, at], dst_ref=dst.at[y, at],
            send_sem=sends.at[step - 1, i], recv_sem=recvs.at[step - 1, i],
            device_id=(dp, peer), device_id_type=MESH,
        )

    own = pltpu.make_async_copy(staged.at[y], from_y.at[y], local_y)
    own.start()
    for i in range(3):
        for step in range(1, N_TENSOR):
            y_copy(staged, from_y, step, i, send_y, recv_y).start()
    own.wait()

    def band_copy(i, k):
        j = tile_at(i)[0] * 4 + k
        return pltpu.make_async_remote_copy(
            src_ref=bands.at[j], dst_ref=rows.at[slot], send_sem=send_p.at[i, k], recv_sem=recv_p.at[z // 4],
            device_id=(home(j) * 2 + core, y), device_id_type=MESH,
        )

    def stays(i, k):
        return works & (tile_at(i)[0] * 4 + k == mine)

    regroup = one_hot(4 * BAND, lambda o: (o // SUB % 4) * BAND + (o // BAND) * SUB + o % SUB)
    for i in range(3):
        for step in range(1, N_TENSOR):
            y_copy(staged, from_y, step, i, send_y, recv_y).wait_recv()
        t, at = tile_at(i)
        tile = from_y[:, at, :].reshape(4 * BAND, WIDE)
        bands[pl.ds(4 * t, 4)] = permuted(regroup, tile).reshape(4, BAND, WIDE)
        for k in range(4):
            @pl.when(jnp.logical_not(stays(i, k)))
            def _():
                band_copy(i, k).start()

    @pl.when(works)
    def _():
        pltpu.make_async_copy(bands.at[mine], rows.at[slot], recv_p.at[z // 4]).start()

        def quarter(d):
            return (z // 4 + d) % 4

        def bands_of(d):
            return pl.ds(quarter(d) * bands_per, bands_per)

        def upper(c):
            return slice(0, (c + 1) * TILE), slice(c * TILE, (c + 1) * TILE)

        def swap(turn, c):
            over = pl.ds(0, (c + 1) * TILE)
            return pltpu.make_async_remote_copy(
                src_ref=half.at[turn, c, over], dst_ref=other.at[turn, c, over],
                send_sem=send_g.at[turn, c], recv_sem=recv_g.at[turn, c],
                device_id=(dp + 1 - 2 * core, y), device_id_type=MESH,
            )

        def give_half(turn, c, value):
            half[turn, c, upper(c)[0]] = value.astype(bf16)
            swap(turn, c).start()

        def gram_sum(turn):
            for c in (2, 1, 0):
                swap(turn, c).wait()
                over, across = upper(c)
                total[over, across] = half[turn, c, over].astype(f32) + other[turn, c, over].astype(f32)

        def set_gram(scale):
            for c in range(WIDE // TILE):
                over, across = upper(c)
                block = (total[over, across] * scale * scale).astype(bf16)
                gram[over, across] = block
                for r in range(c):
                    gram[across, r * TILE:(r + 1) * TILE] = block[r * TILE:(r + 1) * TILE].T

        def polynomial():
            current = gram[...]
            square = jnp.dot(current, current, preferred_element_type=f32)
            poly[...] = (coef_b * current.astype(f32) + coef_c * square).astype(bf16)

        for ds in ((0,), (1, 3), (2,)):
            for d in ds:
                part = rows.at[bands_of(d)]
                pltpu.make_async_copy(part, part, recv_p.at[quarter(d)]).wait()
                at = pl.multiple_of(quarter(d) * TILE, TILE)
                turned[:, pl.ds(at, TILE)] = rows[bands_of(d)].reshape(TILE, WIDE).T
            for c in (2, 1, 0):
                over, across = upper(c)
                value = total[over, across] if ds[0] else 0.0
                for d in ds:
                    at = pl.multiple_of(quarter(d) * TILE, TILE)
                    right = rows[bands_of(d), :, across].reshape(TILE, TILE)
                    value += jnp.dot(turned[over, pl.ds(at, TILE)], right, preferred_element_type=f32)
                if ds[0] == 2:
                    give_half(0, c, value)
                else:
                    total[over, across] = value

        gram_sum(0)
        diagonal = lax.broadcasted_iota(jnp.int32, (TILE, TILE), 0) == lax.broadcasted_iota(jnp.int32, (TILE, TILE), 1)
        on_diagonal = sum(
            jnp.where(diagonal, total[c * TILE:(c + 1) * TILE, c * TILE:(c + 1) * TILE], 0.0) for c in range(WIDE // TILE)
        )
        squares = jnp.sum(jnp.sum(on_diagonal, axis=1, keepdims=True), axis=0, keepdims=True)
        inverse = 1.0 / (jnp.sqrt(squares) + epsilon)
        set_gram(inverse)
        polynomial()

        for b in range(ROWS // TILE):
            at = slice(b * bands_per, (b + 1) * bands_per)
            current = rows[at].reshape(TILE, WIDE)
            product = jnp.dot(current, poly[...], preferred_element_type=f32)
            mixed = ((coef_a * current.astype(f32) + product) * inverse).astype(bf16)
            mid[at] = mixed.reshape(bands_per, BAND, WIDE)
            turned[:, b * TILE:(b + 1) * TILE] = mixed.T

        for c in (2, 1, 0):
            over, across = upper(c)
            right = mid[:, :, across].reshape(ROWS, TILE)
            give_half(1, c, jnp.dot(turned[over], right, preferred_element_type=f32))
        gram_sum(1)
        set_gram(1.0)
        polynomial()

        rms = jnp.sqrt(squares / (D * HW))
        high = rms.astype(bf16).astype(f32)
        low = rms - high
        def give(peer_x, peer_z):
            return pltpu.make_async_remote_copy(
                src_ref=done.at[peer_z * 4 + peer_x], dst_ref=back.at[mine], send_sem=send_b, recv_sem=recv_b.at[mine // 4],
                device_id=((peer_x * 16 + peer_z) * 2 + core, y), device_id_type=MESH,
            )

        far = [(2, r) for r in (1, 2, 0, 3)]
        sides = [pair for n in range(4) for pair in ((1, 3 - n), (3, n))]
        own = [(0, (z + n) % 4) for n in (2, 3, 1, 0)]
        for ds, peers in (((2,), far), ((1, 3), sides), ((0,), own)):
            current = jnp.concatenate([mid[bands_of(d)].reshape(TILE, WIDE) for d in ds], axis=0)
            lane = lax.broadcasted_iota(jnp.int32, current.shape, 1)
            product = jnp.dot(current, poly[...], preferred_element_type=f32)
            mixed = (coef_a * current.astype(f32) + product) * math.sqrt(max(D, HW))
            mixed = jnp.where(lane == HW, high, jnp.where(lane == HW + 1, low, mixed)).astype(bf16)
            for n, d in enumerate(ds):
                done[bands_of(d)] = mixed[n * TILE:(n + 1) * TILE].reshape(bands_per, BAND, WIDE)
            for n, (d, r) in enumerate(peers):
                for h in (2, 1, 3, 0):
                    if d or n < 3 or h:
                        give((x + h) % 4, quarter(d) * 4 + r).start()

        pltpu.make_async_copy(done.at[slot], back.at[mine], recv_b.at[mine // 4]).start()

    for i in (2, 1, 0):
        t, at = tile_at(i)
        four = back.at[pl.ds(4 * t, 4)]
        pltpu.make_async_copy(four, four, recv_b.at[t]).wait()
        tile = back[pl.ds(4 * t, 4)].reshape(4 * BAND, WIDE)
        to_y[:, at, :] = permuted(regroup, tile).reshape(4, BAND, WIDE)
        for step in range(1, N_TENSOR):
            y_copy(to_y, land, step, i, send_z, recv_z).start()

    own = pltpu.make_async_copy(to_y.at[y], land.at[y], local_z)
    own.start()

    index_m = lax.broadcasted_iota(jnp.int32, (MATS, MATS), 0)
    index_n = lax.broadcasted_iota(jnp.int32, (MATS, MATS), 1)
    owners = owner_in[...].astype(f32)
    owner = jnp.sum(jnp.where(index_m == index_n, owners, 0.0), axis=1, keepdims=True)
    rank = jnp.sum(jnp.where((owner == owners) & (index_n < index_m), 1.0, 0.0), axis=1, keepdims=True)
    owned = owner == dp.astype(f32)

    @pl.when(works)
    def _():
        pltpu.make_async_copy(done.at[pl.ds(0, PLANE - 1)], done.at[pl.ds(0, PLANE - 1)], send_b).wait()

    for i in range(3):
        for k in range(4):
            @pl.when(jnp.logical_not(stays(i, k)))
            def _():
                band_copy(i, k).wait_send()

        for step in range(1, N_TENSOR):
            y_copy(staged, from_y, step, i, send_y, recv_y).wait_send()
    own.wait()
    for i in range(3):
        for step in range(1, N_TENSOR):
            y_copy(to_y, land, step, i, send_z, recv_z).wait()

    to_row = one_hot(MATS * SUB, lambda o: (o % MATS) * SUB + o // MATS)
    by_row = permuted(to_row, land[...].reshape(MATS * SUB, WIDE))
    update_out[...] = jnp.concatenate([by_row[MATS * r:MATS * (r + 1), :HW] for r in range(SUB)], axis=1)
    tail = by_row[:MATS, WIDE - 128:].astype(f32)
    lane = lax.broadcasted_iota(jnp.int32, (MATS, 128), 1) - (HW - (WIDE - 128))
    matrix_rms = jnp.sum(jnp.where((lane == 0) | (lane == 1), tail, 0.0), axis=1, keepdims=True)
    ranks = lax.broadcasted_iota(jnp.int32, (MATS, CAP), 1).astype(f32)
    rms_out[...] = jnp.sum(jnp.where(owned & (rank == ranks), matrix_rms, 0.0), axis=0, keepdims=True)


def write_out(*refs):
    copies = [pltpu.make_async_copy(refs[n], refs[n + 3], refs[6].at[n]) for n in range(3)]
    for copy in copies:
        copy.start()
    for copy in copies:
        copy.wait()


def on_device(grad, momentum, owner):
    dma = pltpu.SemaphoreType.DMA
    band = (BAND, WIDE)
    by_y = (N_TENSOR, PER_Y * SUB, WIDE)
    vmem = pl.BlockSpec(memory_space=pltpu.VMEM)
    shapes = (
        jax.ShapeDtypeStruct(momentum.shape, f32),
        jax.ShapeDtypeStruct(grad.shape, bf16),
        jax.ShapeDtypeStruct((1, CAP), f32),
    )
    results = pl.pallas_call(
        kernel,
        out_shape=shapes,
        in_specs=[pl.BlockSpec(memory_space=pltpu.HBM)] * 3,
        out_specs=[vmem] * 3,
        scratch_shapes=[
            pltpu.VMEM(by_y, bf16),
            pltpu.VMEM(by_y, bf16),
            pltpu.VMEM((PER_Y,) + band, bf16),
            pltpu.VMEM((PLANE,) + band, bf16),
            pltpu.VMEM((WIDE, ROWS), bf16),
            pltpu.VMEM((PLANE,) + band, bf16),
            pltpu.VMEM((PLANE,) + band, bf16),
            pltpu.VMEM((WIDE, WIDE), f32),
            pltpu.VMEM((2, WIDE // TILE, WIDE, TILE), bf16),
            pltpu.VMEM((2, WIDE // TILE, WIDE, TILE), bf16),
            pltpu.VMEM((WIDE, WIDE), bf16),
            pltpu.VMEM((WIDE, WIDE), bf16),
            pltpu.VMEM((PER_Y,) + band, bf16),
            pltpu.VMEM(by_y, bf16),
            pltpu.VMEM(by_y, bf16),
            pltpu.VMEM(grad.shape, bf16),
            pltpu.VMEM(momentum.shape, f32),
            pltpu.VMEM((1, MATS), jnp.int32),
            dma((3, 3)), dma((3, 3)), dma((3, 4)), dma((4,)), dma((2, 3)), dma((2, 3)), dma, dma((3,)),
            dma((3, 3)), dma((3, 3)), dma, dma, dma((3,)),
        ],
        compiler_params=pltpu.CompilerParams(
            collective_id=0, has_side_effects=True, vmem_limit_bytes=40 * 1024 * 1024
        ),
    )(*(pltpu.with_memory_space_constraint(v, pltpu.HBM) for v in (grad, momentum, owner.reshape(1, MATS))))
    return pl.pallas_call(
        write_out,
        out_shape=shapes,
        in_specs=[vmem] * 3,
        out_specs=[pl.BlockSpec(memory_space=pl.ANY)] * 3,
        scratch_shapes=[dma((3,))],
    )(*results)


def solution(mesh):
    return jax.shard_map(
        on_device,
        mesh=mesh,
        in_specs=(P(None, ("dp", "tensor")), P(None, ("dp", "tensor")), P()),
        out_specs=(P(None, ("dp", "tensor")), P(None, ("dp", "tensor")), P("dp", None)),
        check_vma=False,
    )
```

```python
import math

import jax
import jax.numpy as jnp
from jax import lax
from jax.experimental import pallas as pl
from jax.experimental.pallas import tpu as pltpu
from jax.sharding import PartitionSpec as P

HW = 704
WIDE = 768
D = 2048
MATS = 48
CAP = 2
N_DP = 128
N_TENSOR = 4
SUB = 4
PLANE = N_DP // 2
PER_Y = MATS // N_TENSOR
BAND = SUB * N_TENSOR
ROWS = PLANE * BAND
TILE = 256

beta_decay = 0.95
coef_a = 3.4445
coef_b = -4.775
coef_c = 2.0315
epsilon = 1e-07

MESH = pl.DeviceIdType.MESH
f32, bf16 = jnp.float32, jnp.bfloat16


def home(j):
    return (j % 4) * 16 + (j * 4) // 3


def around(i):
    return (i + 1) // 2 if i % 2 else -(i // 2)


def one_hot(size, source):
    out_row = lax.broadcasted_iota(jnp.int32, (size, size), 0)
    in_row = lax.broadcasted_iota(jnp.int32, (size, size), 1)
    return (in_row == source(out_row)).astype(f32).astype(bf16)


def permuted(matrix, value):
    return jnp.dot(matrix, value, preferred_element_type=f32).astype(bf16)


def kernel(
    grad_ref, momentum_ref, owner_ref, momentum_out, update_out, rms_out,
    staged, from_y, bands, rows, turned, mid, done, total, half, other, gram, poly, back, to_y, land,
    grad_in, momentum_in, owner_in,
    send_y, recv_y, send_p, recv_p, send_g, recv_g, send_b, recv_b, send_z, recv_z, local_y, local_z, loads,
):
    dp, y = lax.axis_index("dp"), lax.axis_index("tensor")
    core, place = dp % 2, dp // 2
    x, z = place // 16, place % 16
    slot = z * 4 + x
    mine = (3 * z + 3) // 4
    works = ((mine * 4) // 3 == z) & (mine % 4 == x) & (mine < PER_Y)
    bands_per = TILE // BAND

    fetches = [
        pltpu.make_async_copy(src, dst, loads.at[n])
        for n, (src, dst) in enumerate(((grad_ref, grad_in), (momentum_ref, momentum_in), (owner_ref, owner_in)))
    ]
    for fetch in fetches:
        fetch.start()

    barrier = pltpu.get_barrier_semaphore()
    for step in range(1, N_TENSOR):
        pl.semaphore_signal(barrier, inc=1, device_id=(dp, (y + step) % N_TENSOR), device_id_type=MESH)

    @pl.when(works)
    def _():
        pl.semaphore_signal(barrier, inc=1, device_id=(dp + 1 - 2 * core, y), device_id_type=MESH)

        for n in range(16):
            for h in (2, 1, 3, 0):
                if n < 15 or h:
                    peer = (x + h) % 4 * 16 + (z + 8 + around(n)) % 16
                    pl.semaphore_signal(barrier, inc=1, device_id=(peer * 2 + core, y), device_id_type=MESH)

    @pl.when(jnp.logical_not(works))
    def _():
        for j in range(PER_Y):
            pl.semaphore_signal(barrier, inc=1, device_id=(home(j) * 2 + core, y), device_id_type=MESH)

    for fetch in fetches:
        fetch.wait()

    grad = grad_in[...].astype(f32)
    new_momentum = beta_decay * momentum_in[...] + grad
    momentum_out[...] = new_momentum
    nesterov = (grad + beta_decay * new_momentum).astype(bf16)
    edge = jnp.zeros((MATS, WIDE - HW), bf16)
    by_row = jnp.concatenate(
        [jnp.concatenate([nesterov[:, HW * r:HW * (r + 1)], edge], axis=1) for r in range(SUB)], axis=0
    )
    to_matrix = one_hot(MATS * SUB, lambda o: (o % SUB) * MATS + o // SUB)
    staged[...] = permuted(to_matrix, by_row).reshape(N_TENSOR, PER_Y * SUB, WIDE)

    @pl.when(works)
    def _():
        pl.semaphore_wait(barrier, N_TENSOR - 1 + 1 + PLANE - 1)

    @pl.when(jnp.logical_not(works))
    def _():
        pl.semaphore_wait(barrier, N_TENSOR - 1 + PER_Y)

    def tile_at(i):
        near = jnp.minimum(mine, PER_Y - 1)
        t = (near // 4 + 3 + i * jnp.where(near % 4 >= 2, 1, -1)) % 3
        return t, pl.ds(pl.multiple_of(t * BAND, BAND), BAND)

    def y_copy(src, dst, step, i, sends, recvs):
        peer = (y + step) % N_TENSOR
        at = tile_at(i)[1]
        return pltpu.make_async_remote_copy(
            src_ref=src.at[peer, at], dst_ref=dst.at[y, at],
            send_sem=sends.at[step - 1, i], recv_sem=recvs.at[step - 1, i],
            device_id=(dp, peer), device_id_type=MESH,
        )

    own = pltpu.make_async_copy(staged.at[y], from_y.at[y], local_y)
    own.start()
    for i in range(3):
        for step in (2, 1, 3):
            y_copy(staged, from_y, step, i, send_y, recv_y).start()
    own.wait()

    def band_copy(i, k):
        j = tile_at(i)[0] * 4 + k
        return pltpu.make_async_remote_copy(
            src_ref=bands.at[j], dst_ref=rows.at[slot], send_sem=send_p.at[i, k], recv_sem=recv_p.at[z // 4],
            device_id=(home(j) * 2 + core, y), device_id_type=MESH,
        )

    def stays(i, k):
        return works & (tile_at(i)[0] * 4 + k == mine)

    regroup = one_hot(4 * BAND, lambda o: (o // SUB % 4) * BAND + (o // BAND) * SUB + o % SUB)
    for i in range(3):
        for step in range(1, N_TENSOR):
            y_copy(staged, from_y, step, i, send_y, recv_y).wait_recv()
        t, at = tile_at(i)
        tile = from_y[:, at, :].reshape(4 * BAND, WIDE)
        bands[pl.ds(4 * t, 4)] = permuted(regroup, tile).reshape(4, BAND, WIDE)
        for k in range(4):
            @pl.when(jnp.logical_not(stays(i, k)))
            def _():
                band_copy(i, k).start()

    @pl.when(works)
    def _():
        pltpu.make_async_copy(bands.at[mine], rows.at[slot], recv_p.at[z // 4]).start()

        def quarter(d):
            return (z // 4 + d) % 4

        def bands_of(d):
            return pl.ds(quarter(d) * bands_per, bands_per)

        def upper(c):
            return slice(0, (c + 1) * TILE), slice(c * TILE, (c + 1) * TILE)

        def swap(turn, c):
            over = pl.ds(0, (c + 1) * TILE)
            return pltpu.make_async_remote_copy(
                src_ref=half.at[turn, c, over], dst_ref=other.at[turn, c, over],
                send_sem=send_g.at[turn, c], recv_sem=recv_g.at[turn, c],
                device_id=(dp + 1 - 2 * core, y), device_id_type=MESH,
            )

        def give_half(turn, c, value):
            half[turn, c, upper(c)[0]] = value.astype(bf16)
            swap(turn, c).start()

        def gram_sum(turn):
            for c in (2, 1, 0):
                swap(turn, c).wait()
                over, across = upper(c)
                total[over, across] = half[turn, c, over].astype(f32) + other[turn, c, over].astype(f32)

        def set_gram(scale):
            for c in range(WIDE // TILE):
                over, across = upper(c)
                block = (total[over, across] * scale * scale).astype(bf16)
                gram[over, across] = block
                for r in range(c):
                    gram[across, r * TILE:(r + 1) * TILE] = block[r * TILE:(r + 1) * TILE].T

        def polynomial():
            current = gram[...]
            square = jnp.dot(current, current, preferred_element_type=f32)
            poly[...] = (coef_b * current.astype(f32) + coef_c * square).astype(bf16)

        for ds in ((0,), (1, 3), (2,)):
            for d in ds:
                part = rows.at[bands_of(d)]
                pltpu.make_async_copy(part, part, recv_p.at[quarter(d)]).wait()
                at = pl.multiple_of(quarter(d) * TILE, TILE)
                turned[:, pl.ds(at, TILE)] = rows[bands_of(d)].reshape(TILE, WIDE).T
            for c in (2, 1, 0):
                over, across = upper(c)
                value = total[over, across] if ds[0] else 0.0
                for d in ds:
                    at = pl.multiple_of(quarter(d) * TILE, TILE)
                    right = rows[bands_of(d), :, across].reshape(TILE, TILE)
                    value += jnp.dot(turned[over, pl.ds(at, TILE)], right, preferred_element_type=f32)
                if ds[0] == 2:
                    give_half(0, c, value)
                else:
                    total[over, across] = value

        gram_sum(0)
        diagonal = lax.broadcasted_iota(jnp.int32, (TILE, TILE), 0) == lax.broadcasted_iota(jnp.int32, (TILE, TILE), 1)
        on_diagonal = sum(
            jnp.where(diagonal, total[c * TILE:(c + 1) * TILE, c * TILE:(c + 1) * TILE], 0.0) for c in range(WIDE // TILE)
        )
        squares = jnp.sum(jnp.sum(on_diagonal, axis=1, keepdims=True), axis=0, keepdims=True)
        inverse = 1.0 / (jnp.sqrt(squares) + epsilon)
        set_gram(inverse)
        polynomial()

        for b in range(ROWS // TILE):
            at = slice(b * bands_per, (b + 1) * bands_per)
            current = rows[at].reshape(TILE, WIDE)
            product = jnp.dot(current, poly[...], preferred_element_type=f32)
            mixed = ((coef_a * current.astype(f32) + product) * inverse).astype(bf16)
            mid[at] = mixed.reshape(bands_per, BAND, WIDE)
            turned[:, b * TILE:(b + 1) * TILE] = mixed.T

        for c in (2, 1, 0):
            over, across = upper(c)
            right = mid[:, :, across].reshape(ROWS, TILE)
            give_half(1, c, jnp.dot(turned[over], right, preferred_element_type=f32))
        gram_sum(1)
        set_gram(1.0)
        polynomial()

        rms = jnp.sqrt(squares / (D * HW))
        high = rms.astype(bf16).astype(f32)
        low = rms - high
        def give(peer_x, peer_z):
            return pltpu.make_async_remote_copy(
                src_ref=done.at[peer_z * 4 + peer_x], dst_ref=back.at[mine], send_sem=send_b, recv_sem=recv_b.at[mine // 4],
                device_id=((peer_x * 16 + peer_z) * 2 + core, y), device_id_type=MESH,
            )

        far = [(2, r) for r in (1, 2, 0, 3)]
        sides = [pair for n in range(4) for pair in ((1, 3 - n), (3, n))]
        own = [(0, (z + n) % 4) for n in (2, 3, 1, 0)]
        for ds, peers in (((2,), far), ((1, 3), sides), ((0,), own)):
            current = jnp.concatenate([mid[bands_of(d)].reshape(TILE, WIDE) for d in ds], axis=0)
            lane = lax.broadcasted_iota(jnp.int32, current.shape, 1)
            product = jnp.dot(current, poly[...], preferred_element_type=f32)
            mixed = (coef_a * current.astype(f32) + product) * math.sqrt(max(D, HW))
            mixed = jnp.where(lane == HW, high, jnp.where(lane == HW + 1, low, mixed)).astype(bf16)
            for n, d in enumerate(ds):
                done[bands_of(d)] = mixed[n * TILE:(n + 1) * TILE].reshape(bands_per, BAND, WIDE)
            for n, (d, r) in enumerate(peers):
                for h in (2, 1, 3, 0):
                    if d or n < 3 or h:
                        give((x + h) % 4, quarter(d) * 4 + r).start()

        pltpu.make_async_copy(done.at[slot], back.at[mine], recv_b.at[mine // 4]).start()

    for i in (2, 1, 0):
        t, at = tile_at(i)
        four = back.at[pl.ds(4 * t, 4)]
        pltpu.make_async_copy(four, four, recv_b.at[t]).wait()
        tile = back[pl.ds(4 * t, 4)].reshape(4 * BAND, WIDE)
        to_y[:, at, :] = permuted(regroup, tile).reshape(4, BAND, WIDE)
        for step in (2, 1, 3):
            y_copy(to_y, land, step, i, send_z, recv_z).start()

    own = pltpu.make_async_copy(to_y.at[y], land.at[y], local_z)
    own.start()

    index_m = lax.broadcasted_iota(jnp.int32, (MATS, MATS), 0)
    index_n = lax.broadcasted_iota(jnp.int32, (MATS, MATS), 1)
    owners = owner_in[...].astype(f32)
    owner = jnp.sum(jnp.where(index_m == index_n, owners, 0.0), axis=1, keepdims=True)
    rank = jnp.sum(jnp.where((owner == owners) & (index_n < index_m), 1.0, 0.0), axis=1, keepdims=True)
    owned = owner == dp.astype(f32)

    @pl.when(works)
    def _():
        pltpu.make_async_copy(done.at[pl.ds(0, PLANE - 1)], done.at[pl.ds(0, PLANE - 1)], send_b).wait()

    for i in range(3):
        for k in range(4):
            @pl.when(jnp.logical_not(stays(i, k)))
            def _():
                band_copy(i, k).wait_send()

        for step in range(1, N_TENSOR):
            y_copy(staged, from_y, step, i, send_y, recv_y).wait_send()
    own.wait()
    for i in range(3):
        for step in range(1, N_TENSOR):
            y_copy(to_y, land, step, i, send_z, recv_z).wait()

    to_row = one_hot(MATS * SUB, lambda o: (o % MATS) * SUB + o // MATS)
    by_row = permuted(to_row, land[...].reshape(MATS * SUB, WIDE))
    update_out[...] = jnp.concatenate([by_row[MATS * r:MATS * (r + 1), :HW] for r in range(SUB)], axis=1)
    tail = by_row[:MATS, WIDE - 128:].astype(f32)
    lane = lax.broadcasted_iota(jnp.int32, (MATS, 128), 1) - (HW - (WIDE - 128))
    matrix_rms = jnp.sum(jnp.where((lane == 0) | (lane == 1), tail, 0.0), axis=1, keepdims=True)
    ranks = lax.broadcasted_iota(jnp.int32, (MATS, CAP), 1).astype(f32)
    rms_out[...] = jnp.sum(jnp.where(owned & (rank == ranks), matrix_rms, 0.0), axis=0, keepdims=True)


def on_device(grad, momentum, owner):
    dma = pltpu.SemaphoreType.DMA
    band = (BAND, WIDE)
    by_y = (N_TENSOR, PER_Y * SUB, WIDE)
    vmem = pl.BlockSpec(memory_space=pltpu.VMEM)
    return pl.pallas_call(
        kernel,
        out_shape=(
            jax.ShapeDtypeStruct(momentum.shape, f32),
            jax.ShapeDtypeStruct(grad.shape, bf16),
            jax.ShapeDtypeStruct((1, CAP), f32),
        ),
        in_specs=[pl.BlockSpec(memory_space=pltpu.HBM)] * 3,
        out_specs=[vmem] * 3,
        scratch_shapes=[
            pltpu.VMEM(by_y, bf16),
            pltpu.VMEM(by_y, bf16),
            pltpu.VMEM((PER_Y,) + band, bf16),
            pltpu.VMEM((PLANE,) + band, bf16),
            pltpu.VMEM((WIDE, ROWS), bf16),
            pltpu.VMEM((PLANE,) + band, bf16),
            pltpu.VMEM((PLANE,) + band, bf16),
            pltpu.VMEM((WIDE, WIDE), f32),
            pltpu.VMEM((2, WIDE // TILE, WIDE, TILE), bf16),
            pltpu.VMEM((2, WIDE // TILE, WIDE, TILE), bf16),
            pltpu.VMEM((WIDE, WIDE), bf16),
            pltpu.VMEM((WIDE, WIDE), bf16),
            pltpu.VMEM((PER_Y,) + band, bf16),
            pltpu.VMEM(by_y, bf16),
            pltpu.VMEM(by_y, bf16),
            pltpu.VMEM(grad.shape, bf16),
            pltpu.VMEM(momentum.shape, f32),
            pltpu.VMEM((1, MATS), jnp.int32),
            dma((3, 3)), dma((3, 3)), dma((3, 4)), dma((4,)), dma((2, 3)), dma((2, 3)), dma, dma((3,)),
            dma((3, 3)), dma((3, 3)), dma, dma, dma((3,)),
        ],
        compiler_params=pltpu.CompilerParams(
            collective_id=0, has_side_effects=True, vmem_limit_bytes=40 * 1024 * 1024
        ),
    )(*(pltpu.with_memory_space_constraint(v, pltpu.HBM) for v in (grad, momentum, owner.reshape(1, MATS))))


def solution(mesh):
    return jax.shard_map(
        on_device,
        mesh=mesh,
        in_specs=(P(None, ("dp", "tensor")), P(None, ("dp", "tensor")), P()),
        out_specs=(P(None, ("dp", "tensor")), P(None, ("dp", "tensor")), P("dp", None)),
        check_vma=False,
    )
```

```python
import math

import jax
import jax.numpy as jnp
from jax import lax
from jax.experimental import pallas as pl
from jax.experimental.pallas import tpu as pltpu
from jax.sharding import PartitionSpec as P

HW = 704
WIDE = 768
D = 2048
MATS = 48
CAP = 2
N_DP = 128
N_TENSOR = 4
SUB = 4
PLANE = N_DP // 2
PER_Y = MATS // N_TENSOR
BAND = SUB * N_TENSOR
ROWS = PLANE * BAND
TILE = 256

beta_decay = 0.95
coef_a = 3.4445
coef_b = -4.775
coef_c = 2.0315
epsilon = 1e-07

MESH = pl.DeviceIdType.MESH
f32, bf16 = jnp.float32, jnp.bfloat16


def home(j):
    return (j % 4) * 16 + (j * 4) // 3


def around(i):
    return (i + 1) // 2 if i % 2 else -(i // 2)


def one_hot(size, source):
    out_row = lax.broadcasted_iota(jnp.int32, (size, size), 0)
    in_row = lax.broadcasted_iota(jnp.int32, (size, size), 1)
    return (in_row == source(out_row)).astype(f32).astype(bf16)


def permuted(matrix, value):
    return jnp.dot(matrix, value, preferred_element_type=f32).astype(bf16)


def kernel(
    grad_ref, momentum_ref, owner_ref, momentum_out, update_out, rms_out,
    staged, from_y, bands, rows, turned, mid, done, total, half, other, gram, poly, back, to_y, land,
    grad_in, momentum_in, owner_in,
    send_y, recv_y, send_p, recv_p, send_g, recv_g, send_b, recv_b, send_z, recv_z, local_y, local_z, loads,
):
    dp, y = lax.axis_index("dp"), lax.axis_index("tensor")
    core, place = dp % 2, dp // 2
    x, z = place // 16, place % 16
    slot = z * 4 + x
    mine = (3 * z + 3) // 4
    works = ((mine * 4) // 3 == z) & (mine % 4 == x) & (mine < PER_Y)
    bands_per = TILE // BAND

    fetches = [
        pltpu.make_async_copy(src, dst, loads.at[n])
        for n, (src, dst) in enumerate(((grad_ref, grad_in), (momentum_ref, momentum_in), (owner_ref, owner_in)))
    ]
    for fetch in fetches:
        fetch.start()

    barrier = pltpu.get_barrier_semaphore()
    for step in range(1, N_TENSOR):
        pl.semaphore_signal(barrier, inc=1, device_id=(dp, (y + step) % N_TENSOR), device_id_type=MESH)

    @pl.when(works)
    def _():
        pl.semaphore_signal(barrier, inc=1, device_id=(dp + 1 - 2 * core, y), device_id_type=MESH)

        for n in range(16):
            for h in (2, 1, 3, 0):
                if n < 15 or h:
                    peer = (x + h) % 4 * 16 + (z + 8 + around(n)) % 16
                    pl.semaphore_signal(barrier, inc=1, device_id=(peer * 2 + core, y), device_id_type=MESH)

    @pl.when(jnp.logical_not(works))
    def _():
        for j in range(PER_Y):
            pl.semaphore_signal(barrier, inc=1, device_id=(home(j) * 2 + core, y), device_id_type=MESH)

    for fetch in fetches:
        fetch.wait()

    grad = grad_in[...].astype(f32)
    new_momentum = beta_decay * momentum_in[...] + grad
    momentum_out[...] = new_momentum
    nesterov = (grad + beta_decay * new_momentum).astype(bf16)
    edge = jnp.zeros((MATS, WIDE - HW), bf16)
    by_row = jnp.concatenate(
        [jnp.concatenate([nesterov[:, HW * r:HW * (r + 1)], edge], axis=1) for r in range(SUB)], axis=0
    )
    to_matrix = one_hot(MATS * SUB, lambda o: (o % SUB) * MATS + o // SUB)
    staged[...] = permuted(to_matrix, by_row).reshape(N_TENSOR, PER_Y * SUB, WIDE)

    @pl.when(works)
    def _():
        pl.semaphore_wait(barrier, N_TENSOR - 1 + 1 + PLANE - 1)

    @pl.when(jnp.logical_not(works))
    def _():
        pl.semaphore_wait(barrier, N_TENSOR - 1 + PER_Y)

    def tile_at(i):
        near = jnp.minimum(mine, PER_Y - 1)
        t = (near // 4 + 3 + i * jnp.where(near % 4 >= 2, 1, -1)) % 3
        return t, pl.ds(pl.multiple_of(t * BAND, BAND), BAND)

    def y_copy(src, dst, step, i, sends, recvs):
        peer = (y + step) % N_TENSOR
        at = tile_at(i)[1]
        return pltpu.make_async_remote_copy(
            src_ref=src.at[peer, at], dst_ref=dst.at[y, at],
            send_sem=sends.at[step - 1, i], recv_sem=recvs.at[step - 1, i],
            device_id=(dp, peer), device_id_type=MESH,
        )

    for i in range(3):
        for step in (2, 1, 3):
            y_copy(staged, from_y, step, i, send_y, recv_y).start()
    own = pltpu.make_async_copy(staged.at[y], from_y.at[y], local_y)
    own.start()
    own.wait()

    def band_copy(i, k):
        j = tile_at(i)[0] * 4 + k
        return pltpu.make_async_remote_copy(
            src_ref=bands.at[j], dst_ref=rows.at[slot], send_sem=send_p.at[i, k], recv_sem=recv_p.at[z // 4],
            device_id=(home(j) * 2 + core, y), device_id_type=MESH,
        )

    def stays(i, k):
        return works & (tile_at(i)[0] * 4 + k == mine)

    regroup = one_hot(4 * BAND, lambda o: (o // SUB % 4) * BAND + (o // BAND) * SUB + o % SUB)
    for i in range(3):
        for step in range(1, N_TENSOR):
            y_copy(staged, from_y, step, i, send_y, recv_y).wait_recv()
        t, at = tile_at(i)
        tile = from_y[:, at, :].reshape(4 * BAND, WIDE)
        bands[pl.ds(4 * t, 4)] = permuted(regroup, tile).reshape(4, BAND, WIDE)
        for k in range(4):
            @pl.when(jnp.logical_not(stays(i, k)))
            def _():
                band_copy(i, k).start()

    @pl.when(works)
    def _():
        pltpu.make_async_copy(bands.at[mine], rows.at[slot], recv_p.at[z // 4]).start()

        def quarter(d):
            return (z // 4 + d) % 4

        def bands_of(d):
            return pl.ds(quarter(d) * bands_per, bands_per)

        def upper(c):
            return slice(0, (c + 1) * TILE), slice(c * TILE, (c + 1) * TILE)

        def swap(turn, c):
            over = pl.ds(0, (c + 1) * TILE)
            return pltpu.make_async_remote_copy(
                src_ref=half.at[turn, c, over], dst_ref=other.at[turn, c, over],
                send_sem=send_g.at[turn, c], recv_sem=recv_g.at[turn, c],
                device_id=(dp + 1 - 2 * core, y), device_id_type=MESH,
            )

        def give_half(turn, c, value):
            half[turn, c, upper(c)[0]] = value.astype(bf16)
            swap(turn, c).start()

        def whole(turn, c):
            swap(turn, c).wait()
            over = upper(c)[0]
            return half[turn, c, over].astype(f32) + other[turn, c, over].astype(f32)

        def set_gram(c, value):
            over, across = upper(c)
            block = value.astype(bf16)
            gram[over, across] = block
            for r in range(c):
                gram[across, r * TILE:(r + 1) * TILE] = block[r * TILE:(r + 1) * TILE].T

        def polynomial():
            current = gram[...]
            square = jnp.dot(current, current, preferred_element_type=f32)
            poly[...] = (coef_b * current.astype(f32) + coef_c * square).astype(bf16)

        for ds in ((0,), (1, 3), (2,)):
            for d in ds:
                part = rows.at[bands_of(d)]
                pltpu.make_async_copy(part, part, recv_p.at[quarter(d)]).wait()
                at = pl.multiple_of(quarter(d) * TILE, TILE)
                turned[:, pl.ds(at, TILE)] = rows[bands_of(d)].reshape(TILE, WIDE).T
            for c in (2, 1, 0):
                over, across = upper(c)
                value = total[over, across] if ds[0] else 0.0
                for d in ds:
                    at = pl.multiple_of(quarter(d) * TILE, TILE)
                    right = rows[bands_of(d), :, across].reshape(TILE, TILE)
                    value += jnp.dot(turned[over, pl.ds(at, TILE)], right, preferred_element_type=f32)
                if ds[0] == 2:
                    give_half(0, c, value)
                else:
                    total[over, across] = value

        for c in (2, 1, 0):
            total[upper(c)] = whole(0, c)
        diagonal = lax.broadcasted_iota(jnp.int32, (TILE, TILE), 0) == lax.broadcasted_iota(jnp.int32, (TILE, TILE), 1)
        on_diagonal = sum(
            jnp.where(diagonal, total[c * TILE:(c + 1) * TILE, c * TILE:(c + 1) * TILE], 0.0) for c in range(WIDE // TILE)
        )
        squares = jnp.sum(jnp.sum(on_diagonal, axis=1, keepdims=True), axis=0, keepdims=True)
        inverse = 1.0 / (jnp.sqrt(squares) + epsilon)
        for c in range(WIDE // TILE):
            set_gram(c, total[upper(c)] * inverse * inverse)
        polynomial()

        for b in range(ROWS // TILE):
            at = slice(b * bands_per, (b + 1) * bands_per)
            current = rows[at].reshape(TILE, WIDE)
            product = jnp.dot(current, poly[...], preferred_element_type=f32)
            mixed = ((coef_a * current.astype(f32) + product) * inverse).astype(bf16)
            mid[at] = mixed.reshape(bands_per, BAND, WIDE)
            turned[:, b * TILE:(b + 1) * TILE] = mixed.T

        for c in (2, 1, 0):
            over, across = upper(c)
            right = mid[:, :, across].reshape(ROWS, TILE)
            give_half(1, c, jnp.dot(turned[over], right, preferred_element_type=f32))
        for c in (2, 1, 0):
            set_gram(c, whole(1, c))
        polynomial()

        rms = jnp.sqrt(squares / (D * HW))
        high = rms.astype(bf16).astype(f32)
        low = rms - high
        def give(peer_x, peer_z):
            return pltpu.make_async_remote_copy(
                src_ref=done.at[peer_z * 4 + peer_x], dst_ref=back.at[mine], send_sem=send_b, recv_sem=recv_b.at[mine // 4],
                device_id=((peer_x * 16 + peer_z) * 2 + core, y), device_id_type=MESH,
            )

        far = [(2, r) for r in (1, 2, 0, 3)]
        sides = [pair for n in range(4) for pair in ((1, 3 - n), (3, n))]
        own = [(0, (z + n) % 4) for n in (2, 3, 1, 0)]
        for ds, peers in (((2,), far), ((1, 3), sides), ((0,), own)):
            current = jnp.concatenate([mid[bands_of(d)].reshape(TILE, WIDE) for d in ds], axis=0)
            lane = lax.broadcasted_iota(jnp.int32, current.shape, 1)
            product = jnp.dot(current, poly[...], preferred_element_type=f32)
            mixed = (coef_a * current.astype(f32) + product) * math.sqrt(max(D, HW))
            mixed = jnp.where(lane == HW, high, jnp.where(lane == HW + 1, low, mixed)).astype(bf16)
            for n, d in enumerate(ds):
                done[bands_of(d)] = mixed[n * TILE:(n + 1) * TILE].reshape(bands_per, BAND, WIDE)
            for n, (d, r) in enumerate(peers):
                for h in (2, 1, 3, 0):
                    if d or n < 3 or h:
                        give((x + h) % 4, quarter(d) * 4 + r).start()

        pltpu.make_async_copy(done.at[slot], back.at[mine], recv_b.at[mine // 4]).start()

    for i in (2, 1, 0):
        t, at = tile_at(i)
        four = back.at[pl.ds(4 * t, 4)]
        pltpu.make_async_copy(four, four, recv_b.at[t]).wait()
        tile = back[pl.ds(4 * t, 4)].reshape(4 * BAND, WIDE)
        to_y[:, at, :] = permuted(regroup, tile).reshape(4, BAND, WIDE)
        for step in (2, 1, 3):
            y_copy(to_y, land, step, i, send_z, recv_z).start()

    own = pltpu.make_async_copy(to_y.at[y], land.at[y], local_z)
    own.start()

    index_m = lax.broadcasted_iota(jnp.int32, (MATS, MATS), 0)
    index_n = lax.broadcasted_iota(jnp.int32, (MATS, MATS), 1)
    owners = owner_in[...].astype(f32)
    owner = jnp.sum(jnp.where(index_m == index_n, owners, 0.0), axis=1, keepdims=True)
    rank = jnp.sum(jnp.where((owner == owners) & (index_n < index_m), 1.0, 0.0), axis=1, keepdims=True)
    owned = owner == dp.astype(f32)

    @pl.when(works)
    def _():
        pltpu.make_async_copy(done.at[pl.ds(0, PLANE - 1)], done.at[pl.ds(0, PLANE - 1)], send_b).wait()

    for i in range(3):
        for k in range(4):
            @pl.when(jnp.logical_not(stays(i, k)))
            def _():
                band_copy(i, k).wait_send()

        for step in range(1, N_TENSOR):
            y_copy(staged, from_y, step, i, send_y, recv_y).wait_send()
    own.wait()
    for i in range(3):
        for step in range(1, N_TENSOR):
            y_copy(to_y, land, step, i, send_z, recv_z).wait()

    to_row = one_hot(MATS * SUB, lambda o: (o % MATS) * SUB + o // MATS)
    by_row = permuted(to_row, land[...].reshape(MATS * SUB, WIDE))
    update_out[...] = jnp.concatenate([by_row[MATS * r:MATS * (r + 1), :HW] for r in range(SUB)], axis=1)
    tail = by_row[:MATS, WIDE - 128:].astype(f32)
    lane = lax.broadcasted_iota(jnp.int32, (MATS, 128), 1) - (HW - (WIDE - 128))
    matrix_rms = jnp.sum(jnp.where((lane == 0) | (lane == 1), tail, 0.0), axis=1, keepdims=True)
    ranks = lax.broadcasted_iota(jnp.int32, (MATS, CAP), 1).astype(f32)
    rms_out[...] = jnp.sum(jnp.where(owned & (rank == ranks), matrix_rms, 0.0), axis=0, keepdims=True)


def on_device(grad, momentum, owner):
    dma = pltpu.SemaphoreType.DMA
    band = (BAND, WIDE)
    by_y = (N_TENSOR, PER_Y * SUB, WIDE)
    vmem = pl.BlockSpec(memory_space=pltpu.VMEM)
    return pl.pallas_call(
        kernel,
        out_shape=(
            jax.ShapeDtypeStruct(momentum.shape, f32),
            jax.ShapeDtypeStruct(grad.shape, bf16),
            jax.ShapeDtypeStruct((1, CAP), f32),
        ),
        in_specs=[pl.BlockSpec(memory_space=pltpu.HBM)] * 3,
        out_specs=[vmem] * 3,
        scratch_shapes=[
            pltpu.VMEM(by_y, bf16),
            pltpu.VMEM(by_y, bf16),
            pltpu.VMEM((PER_Y,) + band, bf16),
            pltpu.VMEM((PLANE,) + band, bf16),
            pltpu.VMEM((WIDE, ROWS), bf16),
            pltpu.VMEM((PLANE,) + band, bf16),
            pltpu.VMEM((PLANE,) + band, bf16),
            pltpu.VMEM((WIDE, WIDE), f32),
            pltpu.VMEM((2, WIDE // TILE, WIDE, TILE), bf16),
            pltpu.VMEM((2, WIDE // TILE, WIDE, TILE), bf16),
            pltpu.VMEM((WIDE, WIDE), bf16),
            pltpu.VMEM((WIDE, WIDE), bf16),
            pltpu.VMEM((PER_Y,) + band, bf16),
            pltpu.VMEM(by_y, bf16),
            pltpu.VMEM(by_y, bf16),
            pltpu.VMEM(grad.shape, bf16),
            pltpu.VMEM(momentum.shape, f32),
            pltpu.VMEM((1, MATS), jnp.int32),
            dma((3, 3)), dma((3, 3)), dma((3, 4)), dma((4,)), dma((2, 3)), dma((2, 3)), dma, dma((3,)),
            dma((3, 3)), dma((3, 3)), dma, dma, dma((3,)),
        ],
        compiler_params=pltpu.CompilerParams(
            collective_id=0, has_side_effects=True, vmem_limit_bytes=40 * 1024 * 1024
        ),
    )(*(pltpu.with_memory_space_constraint(v, pltpu.HBM) for v in (grad, momentum, owner.reshape(1, MATS))))


def solution(mesh):
    return jax.shard_map(
        on_device,
        mesh=mesh,
        in_specs=(P(None, ("dp", "tensor")), P(None, ("dp", "tensor")), P()),
        out_specs=(P(None, ("dp", "tensor")), P(None, ("dp", "tensor")), P("dp", None)),
        check_vma=False,
    )
```

```python
import math

import jax
import jax.numpy as jnp
from jax import lax
from jax.experimental import pallas as pl
from jax.experimental.pallas import tpu as pltpu
from jax.sharding import PartitionSpec as P

HW = 704
WIDE = 768
D = 2048
MATS = 48
CAP = 2
N_DP = 128
N_TENSOR = 4
SUB = 4
PLANE = N_DP // 2
PER_Y = MATS // N_TENSOR
BAND = SUB * N_TENSOR
ROWS = PLANE * BAND
TILE = 256

beta_decay = 0.95
coef_a = 3.4445
coef_b = -4.775
coef_c = 2.0315
epsilon = 1e-07

MESH = pl.DeviceIdType.MESH
f32, bf16 = jnp.float32, jnp.bfloat16


def home(j):
    return (j % 4) * 16 + (j * 4) // 3


def around(i):
    return (i + 1) // 2 if i % 2 else -(i // 2)


def one_hot(size, source):
    out_row = lax.broadcasted_iota(jnp.int32, (size, size), 0)
    in_row = lax.broadcasted_iota(jnp.int32, (size, size), 1)
    return (in_row == source(out_row)).astype(f32).astype(bf16)


def permuted(matrix, value):
    return jnp.dot(matrix, value, preferred_element_type=f32).astype(bf16)


def kernel(
    grad_ref, momentum_ref, owner_ref, momentum_out, update_out, rms_out,
    staged, from_y, bands, rows, turned, mid, done, total, half, other, gram, poly, back, to_y, land,
    grad_in, momentum_in, owner_in,
    send_y, recv_y, send_p, recv_p, send_g, recv_g, send_b, recv_b, send_z, recv_z, local_y, local_z, loads,
):
    dp, y = lax.axis_index("dp"), lax.axis_index("tensor")
    core, place = dp % 2, dp // 2
    x, z = place // 16, place % 16
    slot = z * 4 + x
    mine = (3 * z + 3) // 4
    works = ((mine * 4) // 3 == z) & (mine % 4 == x) & (mine < PER_Y)
    bands_per = TILE // BAND

    fetches = [
        pltpu.make_async_copy(src, dst, loads.at[n])
        for n, (src, dst) in enumerate(((grad_ref, grad_in), (momentum_ref, momentum_in), (owner_ref, owner_in)))
    ]
    for fetch in fetches:
        fetch.start()

    barrier = pltpu.get_barrier_semaphore()
    for step in range(1, N_TENSOR):
        pl.semaphore_signal(barrier, inc=1, device_id=(dp, (y + step) % N_TENSOR), device_id_type=MESH)

    @pl.when(works)
    def _():
        pl.semaphore_signal(barrier, inc=1, device_id=(dp + 1 - 2 * core, y), device_id_type=MESH)

        for n in range(16):
            for h in (2, 1, 3, 0):
                if n < 15 or h:
                    peer = (x + h) % 4 * 16 + (z + 8 + around(n)) % 16
                    pl.semaphore_signal(barrier, inc=1, device_id=(peer * 2 + core, y), device_id_type=MESH)

    @pl.when(jnp.logical_not(works))
    def _():
        for j in range(PER_Y):
            pl.semaphore_signal(barrier, inc=1, device_id=(home(j) * 2 + core, y), device_id_type=MESH)

    for fetch in fetches:
        fetch.wait()

    grad = grad_in[...].astype(f32)
    new_momentum = beta_decay * momentum_in[...] + grad
    momentum_out[...] = new_momentum
    nesterov = (grad + beta_decay * new_momentum).astype(bf16)
    edge = jnp.zeros((MATS, WIDE - HW), bf16)
    by_row = jnp.concatenate(
        [jnp.concatenate([nesterov[:, HW * r:HW * (r + 1)], edge], axis=1) for r in range(SUB)], axis=0
    )
    to_matrix = one_hot(MATS * SUB, lambda o: (o % SUB) * MATS + o // SUB)
    staged[...] = permuted(to_matrix, by_row).reshape(N_TENSOR, PER_Y * SUB, WIDE)

    @pl.when(works)
    def _():
        pl.semaphore_wait(barrier, N_TENSOR - 1 + 1 + PLANE - 1)

    @pl.when(jnp.logical_not(works))
    def _():
        pl.semaphore_wait(barrier, N_TENSOR - 1 + PER_Y)

    def tile_at(i):
        near = jnp.minimum(mine, PER_Y - 1)
        t = (near // 4 + 3 + i * jnp.where(near % 4 >= 2, 1, -1)) % 3
        return t, pl.ds(pl.multiple_of(t * BAND, BAND), BAND)

    def y_copy(src, dst, step, i, sends, recvs):
        peer = (y + step) % N_TENSOR
        at = tile_at(i)[1]
        return pltpu.make_async_remote_copy(
            src_ref=src.at[peer, at], dst_ref=dst.at[y, at],
            send_sem=sends.at[step - 1, i], recv_sem=recvs.at[step - 1, i],
            device_id=(dp, peer), device_id_type=MESH,
        )

    for i in range(3):
        for step in (2, 1, 3):
            y_copy(staged, from_y, step, i, send_y, recv_y).start()
    own = pltpu.make_async_copy(staged.at[y], from_y.at[y], local_y)
    own.start()
    own.wait()

    def band_copy(i, k):
        j = tile_at(i)[0] * 4 + k
        return pltpu.make_async_remote_copy(
            src_ref=bands.at[j], dst_ref=rows.at[slot], send_sem=send_p.at[i, k], recv_sem=recv_p.at[z // 4],
            device_id=(home(j) * 2 + core, y), device_id_type=MESH,
        )

    def stays(i, k):
        return works & (tile_at(i)[0] * 4 + k == mine)

    regroup = one_hot(4 * BAND, lambda o: (o // SUB % 4) * BAND + (o // BAND) * SUB + o % SUB)
    for i in range(3):
        for step in range(1, N_TENSOR):
            y_copy(staged, from_y, step, i, send_y, recv_y).wait_recv()
        t, at = tile_at(i)
        tile = from_y[:, at, :].reshape(4 * BAND, WIDE)
        bands[pl.ds(4 * t, 4)] = permuted(regroup, tile).reshape(4, BAND, WIDE)
        for k in range(4):
            @pl.when(jnp.logical_not(stays(i, k)))
            def _():
                band_copy(i, k).start()

    @pl.when(works)
    def _():
        pltpu.make_async_copy(bands.at[mine], rows.at[slot], recv_p.at[z // 4]).start()

        def quarter(d):
            return (z // 4 + d) % 4

        def bands_of(d):
            return pl.ds(quarter(d) * bands_per, bands_per)

        def upper(c):
            return slice(0, (c + 1) * TILE), slice(c * TILE, (c + 1) * TILE)

        def swap(turn, c):
            over = pl.ds(0, (c + 1) * TILE)
            return pltpu.make_async_remote_copy(
                src_ref=half.at[turn, c, over], dst_ref=other.at[turn, c, over],
                send_sem=send_g.at[turn, c], recv_sem=recv_g.at[turn, c],
                device_id=(dp + 1 - 2 * core, y), device_id_type=MESH,
            )

        def give_half(turn, c, value):
            half[turn, c, upper(c)[0]] = value.astype(bf16)
            swap(turn, c).start()

        def whole(turn, c):
            swap(turn, c).wait()
            over = upper(c)[0]
            return half[turn, c, over].astype(f32) + other[turn, c, over].astype(f32)

        def set_gram(c, value):
            over, across = upper(c)
            block = value.astype(bf16)
            gram[over, across] = block
            for r in range(c):
                gram[across, r * TILE:(r + 1) * TILE] = block[r * TILE:(r + 1) * TILE].T

        def polynomial():
            current = gram[...]
            square = jnp.dot(current, current, preferred_element_type=f32)
            poly[...] = (coef_b * current.astype(f32) + coef_c * square).astype(bf16)

        for ds in ((0,), (1, 3), (2,)):
            for d in ds:
                part = rows.at[bands_of(d)]
                pltpu.make_async_copy(part, part, recv_p.at[quarter(d)]).wait()
                at = pl.multiple_of(quarter(d) * TILE, TILE)
                turned[:, pl.ds(at, TILE)] = rows[bands_of(d)].reshape(TILE, WIDE).T
            for c in (2, 1, 0):
                over, across = upper(c)
                value = total[over, across] if ds[0] else 0.0
                for d in ds:
                    at = pl.multiple_of(quarter(d) * TILE, TILE)
                    right = rows[bands_of(d), :, across].reshape(TILE, TILE)
                    value += jnp.dot(turned[over, pl.ds(at, TILE)], right, preferred_element_type=f32)
                if ds[0] == 2:
                    give_half(0, c, value)
                else:
                    total[over, across] = value

        for c in (2, 1, 0):
            total[upper(c)] = whole(0, c)
        diagonal = lax.broadcasted_iota(jnp.int32, (TILE, TILE), 0) == lax.broadcasted_iota(jnp.int32, (TILE, TILE), 1)
        on_diagonal = sum(
            jnp.where(diagonal, total[c * TILE:(c + 1) * TILE, c * TILE:(c + 1) * TILE], 0.0) for c in range(WIDE // TILE)
        )
        squares = jnp.sum(jnp.sum(on_diagonal, axis=1, keepdims=True), axis=0, keepdims=True)
        inverse = 1.0 / (jnp.sqrt(squares) + epsilon)
        for c in range(WIDE // TILE):
            set_gram(c, total[upper(c)] * inverse * inverse)
        polynomial()

        for b in range(ROWS // TILE):
            at = slice(b * bands_per, (b + 1) * bands_per)
            current = rows[at].reshape(TILE, WIDE)
            product = jnp.dot(current, poly[...], preferred_element_type=f32)
            mixed = ((coef_a * current.astype(f32) + product) * inverse).astype(bf16)
            mid[at] = mixed.reshape(bands_per, BAND, WIDE)
            turned[:, b * TILE:(b + 1) * TILE] = mixed.T

        for c in (2, 1, 0):
            over, across = upper(c)
            right = mid[:, :, across].reshape(ROWS, TILE)
            give_half(1, c, jnp.dot(turned[over], right, preferred_element_type=f32))
        for c in (2, 1, 0):
            set_gram(c, whole(1, c))
        polynomial()

        rms = jnp.sqrt(squares / (D * HW))
        high = rms.astype(bf16).astype(f32)
        low = rms - high
        def give(peer_x, peer_z):
            return pltpu.make_async_remote_copy(
                src_ref=done.at[peer_z * 4 + peer_x], dst_ref=back.at[mine], send_sem=send_b, recv_sem=recv_b.at[mine // 4],
                device_id=((peer_x * 16 + peer_z) * 2 + core, y), device_id_type=MESH,
            )

        far = [(2, r) for r in (1, 2, 0, 3)]
        sides = [pair for n in range(4) for pair in ((1, 3 - n), (3, n))]
        own = [(0, (z + n) % 4) for n in (2, 3, 1, 0)]
        for ds, peers in (((2,), far), ((1, 3), sides), ((0,), own)):
            current = jnp.concatenate([mid[bands_of(d)].reshape(TILE, WIDE) for d in ds], axis=0)
            lane = lax.broadcasted_iota(jnp.int32, current.shape, 1)
            product = jnp.dot(current, poly[...], preferred_element_type=f32)
            mixed = (coef_a * current.astype(f32) + product) * math.sqrt(max(D, HW))
            mixed = jnp.where(lane == HW, high, jnp.where(lane == HW + 1, low, mixed)).astype(bf16)
            for n, d in enumerate(ds):
                done[bands_of(d)] = mixed[n * TILE:(n + 1) * TILE].reshape(bands_per, BAND, WIDE)
            for n, (d, r) in enumerate(peers):
                for h in (2, 1, 3, 0):
                    if d or n < 3 or h:
                        if len(ds) == 2:
                            side = 1 + 2 * ((n + core) % 2)
                            at_z = quarter(side) * 4 + jnp.where(side == 1, 3 - n // 2, n // 2)
                        else:
                            at_z = quarter(d) * 4 + r
                        give((x + 4 + h * (1 - 2 * core)) % 4, at_z).start()

        pltpu.make_async_copy(done.at[slot], back.at[mine], recv_b.at[mine // 4]).start()

    for i in (2, 1, 0):
        t, at = tile_at(i)
        four = back.at[pl.ds(4 * t, 4)]
        pltpu.make_async_copy(four, four, recv_b.at[t]).wait()
        tile = back[pl.ds(4 * t, 4)].reshape(4 * BAND, WIDE)
        to_y[:, at, :] = permuted(regroup, tile).reshape(4, BAND, WIDE)
        for step in (2, 1, 3):
            y_copy(to_y, land, step, i, send_z, recv_z).start()

    own = pltpu.make_async_copy(to_y.at[y], land.at[y], local_z)
    own.start()

    index_m = lax.broadcasted_iota(jnp.int32, (MATS, MATS), 0)
    index_n = lax.broadcasted_iota(jnp.int32, (MATS, MATS), 1)
    owners = owner_in[...].astype(f32)
    owner = jnp.sum(jnp.where(index_m == index_n, owners, 0.0), axis=1, keepdims=True)
    rank = jnp.sum(jnp.where((owner == owners) & (index_n < index_m), 1.0, 0.0), axis=1, keepdims=True)
    owned = owner == dp.astype(f32)

    @pl.when(works)
    def _():
        pltpu.make_async_copy(done.at[pl.ds(0, PLANE - 1)], done.at[pl.ds(0, PLANE - 1)], send_b).wait()

    for i in range(3):
        for k in range(4):
            @pl.when(jnp.logical_not(stays(i, k)))
            def _():
                band_copy(i, k).wait_send()

        for step in range(1, N_TENSOR):
            y_copy(staged, from_y, step, i, send_y, recv_y).wait_send()
    own.wait()
    for i in range(3):
        for step in range(1, N_TENSOR):
            y_copy(to_y, land, step, i, send_z, recv_z).wait()

    to_row = one_hot(MATS * SUB, lambda o: (o % MATS) * SUB + o // MATS)
    by_row = permuted(to_row, land[...].reshape(MATS * SUB, WIDE))
    update_out[...] = jnp.concatenate([by_row[MATS * r:MATS * (r + 1), :HW] for r in range(SUB)], axis=1)
    tail = by_row[:MATS, WIDE - 128:].astype(f32)
    lane = lax.broadcasted_iota(jnp.int32, (MATS, 128), 1) - (HW - (WIDE - 128))
    matrix_rms = jnp.sum(jnp.where((lane == 0) | (lane == 1), tail, 0.0), axis=1, keepdims=True)
    ranks = lax.broadcasted_iota(jnp.int32, (MATS, CAP), 1).astype(f32)
    rms_out[...] = jnp.sum(jnp.where(owned & (rank == ranks), matrix_rms, 0.0), axis=0, keepdims=True)


def on_device(grad, momentum, owner):
    dma = pltpu.SemaphoreType.DMA
    band = (BAND, WIDE)
    by_y = (N_TENSOR, PER_Y * SUB, WIDE)
    vmem = pl.BlockSpec(memory_space=pltpu.VMEM)
    return pl.pallas_call(
        kernel,
        out_shape=(
            jax.ShapeDtypeStruct(momentum.shape, f32),
            jax.ShapeDtypeStruct(grad.shape, bf16),
            jax.ShapeDtypeStruct((1, CAP), f32),
        ),
        in_specs=[pl.BlockSpec(memory_space=pltpu.HBM)] * 3,
        out_specs=[vmem] * 3,
        scratch_shapes=[
            pltpu.VMEM(by_y, bf16),
            pltpu.VMEM(by_y, bf16),
            pltpu.VMEM((PER_Y,) + band, bf16),
            pltpu.VMEM((PLANE,) + band, bf16),
            pltpu.VMEM((WIDE, ROWS), bf16),
            pltpu.VMEM((PLANE,) + band, bf16),
            pltpu.VMEM((PLANE,) + band, bf16),
            pltpu.VMEM((WIDE, WIDE), f32),
            pltpu.VMEM((2, WIDE // TILE, WIDE, TILE), bf16),
            pltpu.VMEM((2, WIDE // TILE, WIDE, TILE), bf16),
            pltpu.VMEM((WIDE, WIDE), bf16),
            pltpu.VMEM((WIDE, WIDE), bf16),
            pltpu.VMEM((PER_Y,) + band, bf16),
            pltpu.VMEM(by_y, bf16),
            pltpu.VMEM(by_y, bf16),
            pltpu.VMEM(grad.shape, bf16),
            pltpu.VMEM(momentum.shape, f32),
            pltpu.VMEM((1, MATS), jnp.int32),
            dma((3, 3)), dma((3, 3)), dma((3, 4)), dma((4,)), dma((2, 3)), dma((2, 3)), dma, dma((3,)),
            dma((3, 3)), dma((3, 3)), dma, dma, dma((3,)),
        ],
        compiler_params=pltpu.CompilerParams(
            collective_id=0, has_side_effects=True, vmem_limit_bytes=40 * 1024 * 1024
        ),
    )(*(pltpu.with_memory_space_constraint(v, pltpu.HBM) for v in (grad, momentum, owner.reshape(1, MATS))))


def solution(mesh):
    return jax.shard_map(
        on_device,
        mesh=mesh,
        in_specs=(P(None, ("dp", "tensor")), P(None, ("dp", "tensor")), P()),
        out_specs=(P(None, ("dp", "tensor")), P(None, ("dp", "tensor")), P("dp", None)),
        check_vma=False,
    )
```
